128 devices in a mesh: seq: 16 (over y, z), slide: 8 (over x, core).
Axes of the slice: x: 4, y: 4, z: 4, core: 2. Of those that a mesh axis runs over, the one named last changes fastest.
Arguments:
- inputs: bfloat16 [8, 4096, 768], P('slide', 'seq'), may hold values from -6 to 6
- cotangent: bfloat16 [8, 4096, 768], P('slide', 'seq'), may hold values from -6 to 6
- key_tiles: int32 [8, 4, 16, 8], P('slide'), may hold values from 0 to 31, as said below
- tile_valid: int32 [8, 32], P('slide'), may hold values from 0 to 1, as said below
- w_qkv: bfloat16 [768, 2304], replicated, may hold values from -0.21650635 to 0.21650635
- w_out: bfloat16 [768, 768], replicated, may hold values from -0.21875 to 0.21875
Outputs:
- outputs: bfloat16 [8, 4096, 768], P('slide', 'seq')
- grad_inputs: bfloat16 [8, 4096, 768], P('slide', 'seq')
- w_qkv_grad: float32 [768, 2304], P('seq')
- w_out_grad: float32 [768, 768], P('seq')
The draws below stay inside these ranges and needn't reach their ends.
Inputs may be any that keep to these rules, and one draw needn't show every extreme that they name: Row key_tiles[s,g,p] is start + o + i*r for i < 8, with dilation r of 2 or 4 for the group of the slide, 0 <= o < r, and start the first tile of the segment of 8*r tiles that holds block p. At most 1 entry of a row lies in one block of 2 tiles, and every slide has at least one group with dilation 2, whose rows hold exactly one tile of each block of their segment. `tile_valid`: the first tile of every block of 2 tiles is 1.
All inputs are finite; a program needn't handle non-finite values.
Results may differ from the reference program's by a relative error of at most 0.013.
Values may be sent and summed in bfloat16 or wider, within the bound.
No kernel may reach another device: no remote copies, remote signals or barrier semaphores. Data moves between devices by JAX's collectives and lax.ppermute only.
A program may use at most 192 MiB of HBM per device.

```python
import jax
import jax.numpy as jnp
from jax import lax

D = 768
H = 12
G = 4
TILE = 128
C = 2
HD = 64
HPG = 3
SLIDES = 8
NT = 32
KT = 8
TOK = 256
L = 4096
N_SEQ = 16


def draw_inputs(key, part):
    key = jax.random.fold_in(key, 5)
    base_key = jax.random.fold_in(key, 0)
    return jax.random.truncated_normal(base_key, -6.0, 6.0, (SLIDES, L, D), jnp.float32).astype(jnp.bfloat16)


def draw_w_qkv(key, part):
    key = jax.random.fold_in(key, 7)
    noise_key = jax.random.fold_in(key, 0)
    return (jax.random.truncated_normal(noise_key, -6.0, 6.0, (D, 3 * D), jnp.float32) * D ** (-0.5)).astype(jnp.bfloat16)


def draw_key_tiles(key, part):
    key = jax.random.fold_in(key, 11)
    rate_key, force_key, offset_key = jax.random.split(key, 3)
    wide = jax.random.randint(rate_key, (SLIDES, G), 0, 2)
    forced = jax.random.randint(force_key, (SLIDES, 1), 0, G)
    wide = jnp.where(jnp.arange(G)[None, :] == forced, 0, wide)
    stride = 2 + 2 * wide
    offset = jax.random.randint(offset_key, (SLIDES, G), 0, 4) % stride
    span = KT * stride
    reader = jnp.arange(NT // C)
    start = reader[None, None, :] * C // span[..., None] * span[..., None]
    lists = start[..., None] + offset[..., None, None] + jnp.arange(KT)[None, None, None, :] * stride[..., None, None]
    return lists.astype(jnp.int32)


def draw_tile_valid(key, part):
    key = jax.random.fold_in(key, 23)
    draws = jax.random.randint(key, (SLIDES, NT), 0, 10)
    first = (jnp.arange(NT) % C == 0)[None, :]
    return jnp.where(first | (draws < 7), 1, 0).astype(jnp.int32)


def block_scale(own_key, shape, shards, smallest, top_value):
    def one(position, parts):
        steps = jax.random.uniform(jax.random.fold_in(jax.random.fold_in(own_key, 6), position), (parts,), jnp.float32, smallest / len(shards), top_value / len(shards))
        return jnp.repeat(jnp.exp(steps), shape[position] // parts).reshape((-1,) + (1,) * (len(shape) - position - 1))

    level = one(*shards[0])
    for cut in shards[1:]:
        level = level * one(*cut)
    return level


def scatter_about(rng, dims, scale, most, cuts=(), held_as=jnp.bfloat16):
    values = jax.random.normal(rng, dims, jnp.float32) * scale
    if len(cuts) > 0:
        values = block_scale(rng, dims, cuts, -0.22, 0.18) * values
    return jnp.clip(values, min=-most, max=most).astype(held_as)


def setup_inputs(seed: int = 0) -> dict:
    seeds = jax.random.split(jax.random.key(seed), 7)
    inputs = draw_inputs(jax.random.fold_in(seeds[6], 71), 0)
    cotangent = scatter_about(seeds[1], (SLIDES, L, D), 1.0, 6.0, ((0, 8), (1, 16)))
    key_tiles = draw_key_tiles(jax.random.fold_in(seeds[6], 71), 0)
    tile_valid = draw_tile_valid(jax.random.fold_in(seeds[6], 71), 0)
    w_qkv = draw_w_qkv(jax.random.fold_in(seeds[6], 71), 0)
    w_out = scatter_about(seeds[5], (D, D), D ** -0.5, 0.21875)
    return {"inputs": inputs, "cotangent": cotangent, "key_tiles": key_tiles, "tile_valid": tile_valid, "w_qkv": w_qkv, "w_out": w_out}


NEG_FILL = -1.0e30


def to_low(array):
    return lax.optimization_barrier(array.astype(jnp.bfloat16))


def softmax_rows(scores, allowed):
    scores = jnp.where(allowed, scores, NEG_FILL)
    top = jnp.max(scores, axis=-1, keepdims=True)
    expo = jnp.exp(scores - top)
    return expo / jnp.sum(expo, axis=-1, keepdims=True)


def slide_pass(inputs, cotangent, lists, valid, w_qkv, w_out):
    f32 = jnp.float32
    scale = HD ** -0.5
    projected = to_low(jnp.dot(inputs, w_qkv, preferred_element_type=f32))
    queries = projected[:, :D].reshape(NT, TILE, H, HD)
    keys = projected[:, D:2 * D].reshape(NT, TILE, H, HD)
    values = projected[:, 2 * D:].reshape(NT, TILE, H, HD)
    head_group = jnp.arange(H) // HPG
    head_lists = lists[head_group]
    keys_heads = jnp.moveaxis(keys, 2, 0)
    values_heads = jnp.moveaxis(values, 2, 0)

    def pick_far(table, rows):
        return table[rows]

    def per_reader(reader):
        first = (reader * C).astype(jnp.int32)
        query_rows = lax.dynamic_slice_in_dim(queries, first, C, 0).reshape(TOK, H, HD)
        near_keys = lax.dynamic_slice_in_dim(keys, first, C, 0).reshape(TOK, H, HD)
        near_values = lax.dynamic_slice_in_dim(values, first, C, 0).reshape(TOK, H, HD)
        grad_rows = lax.dynamic_slice_in_dim(cotangent, (reader * TOK).astype(jnp.int32), TOK, 0)
        picked = lax.dynamic_index_in_dim(head_lists, reader, 1, keepdims=False)
        far_keys = jax.vmap(pick_far)(keys_heads, picked).reshape(H, KT * TILE, HD)
        far_values = jax.vmap(pick_far)(values_heads, picked).reshape(H, KT * TILE, HD)
        all_keys = jnp.concatenate([near_keys, jnp.moveaxis(far_keys, 0, 1)], 0).astype(f32)
        all_values = jnp.concatenate([near_values, jnp.moveaxis(far_values, 0, 1)], 0).astype(f32)
        near_valid = jnp.repeat(lax.dynamic_slice_in_dim(valid, first, C, 0), TILE)
        far_valid = jnp.repeat(valid[picked], TILE, axis=1)
        allowed = jnp.concatenate([jnp.broadcast_to(near_valid[None, :], (H, TOK)), far_valid], 1) > 0
        query_f = query_rows.astype(f32)
        scores = jnp.einsum('qhd,khd->hqk', query_f, all_keys) * scale
        probs = softmax_rows(scores, allowed[:, None, :])
        probs_low = to_low(probs).astype(f32)
        attended = to_low(jnp.einsum('hqk,khd->qhd', probs_low, all_values))
        flat = attended.reshape(TOK, D)
        out_rows = jnp.dot(flat, w_out, preferred_element_type=f32).astype(jnp.bfloat16)
        grad_attended = to_low(jnp.dot(grad_rows, w_out.T, preferred_element_type=f32))
        grad_f = grad_attended.reshape(TOK, H, HD).astype(f32)
        grad_probs = jnp.einsum('qhd,khd->hqk', grad_f, all_values)
        center = jnp.sum(probs * grad_probs, axis=-1, keepdims=True)
        grad_scores = to_low(probs * (grad_probs - center) * scale).astype(f32)
        grad_query = jnp.einsum('hqk,khd->qhd', grad_scores, all_keys)
        grad_keys = jnp.einsum('hqk,qhd->khd', grad_scores, query_f)
        grad_values = jnp.einsum('hqk,qhd->khd', probs_low, grad_f)
        far_gk = jnp.moveaxis(to_low(grad_keys[TOK:]), 1, 0).reshape(H, KT, TILE, HD)
        far_gv = jnp.moveaxis(to_low(grad_values[TOK:]), 1, 0).reshape(H, KT, TILE, HD)
        return out_rows, flat, grad_query, grad_keys[:TOK], grad_values[:TOK], far_gk, far_gv

    results = lax.map(per_reader, jnp.arange(N_SEQ, dtype=jnp.int32))
    out_rows, flats, grad_query, near_gk, near_gv, far_gk, far_gv = results
    heads_index = jnp.broadcast_to(jnp.arange(H, dtype=jnp.int32)[:, None, None], (H, N_SEQ, KT))

    def spread(near, far):
        total = jnp.moveaxis(near.reshape(NT, TILE, H, HD), 2, 0)
        total = total.at[heads_index, head_lists].add(jnp.moveaxis(far, 0, 1).astype(f32))
        return jnp.moveaxis(total, 0, 2).reshape(L, D)

    grad_proj = to_low(jnp.concatenate([grad_query.reshape(L, D), spread(near_gk, far_gk), spread(near_gv, far_gv)], 1))
    grad_inputs = jnp.dot(grad_proj, w_qkv.T, preferred_element_type=f32).astype(jnp.bfloat16)
    w_qkv_part = jnp.dot(inputs.T, grad_proj, preferred_element_type=f32)
    w_out_part = jnp.dot(flats.reshape(L, D).T, cotangent, preferred_element_type=f32)
    return out_rows.reshape(L, D), grad_inputs, w_qkv_part, w_out_part


def reference(inputs, cotangent, key_tiles, tile_valid, w_qkv, w_out):
    def one_slide(index):
        return slide_pass(inputs[index], cotangent[index], key_tiles[index], tile_valid[index], w_qkv, w_out)

    outputs, grad_inputs, w_qkv_parts, w_out_parts = lax.map(one_slide, jnp.arange(SLIDES, dtype=jnp.int32))
    return outputs, grad_inputs, jnp.sum(w_qkv_parts, 0), jnp.sum(w_out_parts, 0)
```

```python
import jax
import jax.numpy as jnp
from jax import lax
from jax.experimental import pallas as pl
from jax.experimental.pallas import tpu as pltpu
from jax.sharding import PartitionSpec as P

H = 12
HPG = 3
HD = 64
TILE = 128
NEG_FILL = -1e30
F32 = jnp.float32
BF16 = jnp.bfloat16
SCALE = HD ** (-0.5)


def slot_of(head):
    row = head // HPG
    place = head % HPG
    return 4 * row + place + (place >= row)


def project_body(x_ref, cot_ref, wq_ref, wk_ref, wv_ref, wo_ref, out_ref):
    step = pl.program_id(0)
    x = x_ref[...]
    contract = (((0,), (1,)), ((), ()))
    qt = lax.dot_general(wq_ref[...], x, contract, preferred_element_type=F32).astype(BF16)
    kt = lax.dot_general(wk_ref[...], x, contract, preferred_element_type=F32).astype(BF16)
    vt = lax.dot_general(wv_ref[...], x, contract, preferred_element_type=F32).astype(BF16)
    gt = lax.dot_general(
        wo_ref[...], cot_ref[...], (((1,), (1,)), ((), ())), preferred_element_type=F32
    ).astype(BF16)
    qt = qt * jnp.asarray(SCALE, BF16)
    for half in range(2):
        head = 2 * step + half
        row = head // HPG
        place = head - row * HPG
        slot = 4 * row + place + jnp.where(place >= row, 1, 0)
        rows = slice(half * HD, half * HD + HD)
        out_ref[slot, 0:HD, :] = qt[rows]
        out_ref[slot, HD : 2 * HD, :] = kt[rows]
        out_ref[slot, 2 * HD : 3 * HD, :] = vt[rows]
        out_ref[slot, 3 * HD :, :] = gt[rows]

    @pl.when(step == 0)
    def _():
        for row in range(4):
            out_ref[5 * row] = jnp.zeros(out_ref.shape[1:], BF16)


def project(x, cot, w_qkv, w_out):
    tok, width = x.shape
    pairs = H // 2
    return pl.pallas_call(
        project_body,
        grid=(pairs,),
        in_specs=[
            pl.BlockSpec((tok, width), lambda i: (0, 0)),
            pl.BlockSpec((tok, width), lambda i: (0, 0)),
            pl.BlockSpec((width, 2 * HD), lambda i: (0, i)),
            pl.BlockSpec((width, 2 * HD), lambda i: (0, i + pairs)),
            pl.BlockSpec((width, 2 * HD), lambda i: (0, i + 2 * pairs)),
            pl.BlockSpec((2 * HD, width), lambda i: (i, 0)),
        ],
        out_specs=pl.BlockSpec((16, 4 * HD, tok), lambda i: (0, 0, 0)),
        out_shape=jax.ShapeDtypeStruct((16, 4 * HD, tok), BF16),
        compiler_params=pltpu.CompilerParams(vmem_limit_bytes=32 * 2**20),
        cost_estimate=pl.CostEstimate(
            flops=2 * tok * width * 4 * width, bytes_accessed=8 * 2**20, transcendentals=0
        ),
        name="project",
    )(x, cot, w_qkv, w_qkv, w_qkv, w_out)


def attend_body(tiles_ref, valid_ref, in_ref, out_ref, kv, kvt, dkv):
    blocks = in_ref.shape[0]
    listed = tiles_ref.shape[1]

    def prepare(b, carry):
        both = in_ref[b, HD : 3 * HD, :]
        flipped = both.T
        for c in range(2):
            kvt[2 * b + c] = both[:, c * TILE : (c + 1) * TILE]
            kv[2 * b + c] = flipped[c * TILE : (c + 1) * TILE]
            dkv[2 * b + c] = jnp.zeros((TILE, 2 * HD), F32)
        return carry

    lax.fori_loop(0, blocks, prepare, 0)

    def block(b, carry):
        tiles = [2 * b, 2 * b + 1] + [tiles_ref[b, i] for i in range(listed)]
        qt = in_ref[b, 0:HD, :]
        gt = in_ref[b, 3 * HD :, :]
        zero = jnp.zeros_like(qt)
        keys = jnp.concatenate([kv[t] for t in tiles], axis=0)
        scores = jnp.dot(
            keys, jnp.concatenate([qt, zero], axis=0), preferred_element_type=F32
        )
        grad_probs = jnp.dot(
            keys, jnp.concatenate([zero, gt], axis=0), preferred_element_type=F32
        )
        pieces = []
        for i, t in enumerate(tiles):
            bias = jnp.where(valid_ref[t] > 0, 0.0, NEG_FILL).astype(F32)
            pieces.append(scores[i * TILE : (i + 1) * TILE] + bias)
        scores = jnp.concatenate(pieces, axis=0)
        top = jnp.max(scores, axis=0, keepdims=True)
        expo = jnp.exp(scores - top)
        probs = expo * (1.0 / jnp.sum(expo, axis=0, keepdims=True))
        low = probs.astype(BF16)
        keys_t = jnp.concatenate([kvt[t, 0:HD] for t in tiles], axis=1)
        values_t = jnp.concatenate([kvt[t, HD:] for t in tiles], axis=1)
        attended = jnp.dot(values_t, low, preferred_element_type=F32)
        center = jnp.sum(attended * gt.astype(F32), axis=0, keepdims=True)
        grad_scores = (probs * (grad_probs - center)).astype(BF16)
        grad_q = jnp.dot(keys_t, grad_scores, preferred_element_type=F32) * SCALE
        out_ref[b, 0:HD, :] = attended.astype(BF16)
        out_ref[b, HD : 2 * HD, :] = grad_q.astype(BF16)
        flipped = jnp.concatenate([qt, gt], axis=0).T
        lane = lax.broadcasted_iota(jnp.int32, flipped.shape, 1)
        nothing = jnp.zeros_like(flipped)
        right = jnp.concatenate(
            [jnp.where(lane < HD, flipped, nothing), jnp.where(lane < HD, nothing, flipped)],
            axis=0,
        )
        terms = jnp.dot(
            jnp.concatenate([grad_scores, low], axis=1), right, preferred_element_type=F32
        )
        for i, t in enumerate(tiles):
            dkv[t] += terms[i * TILE : (i + 1) * TILE]
        return carry

    lax.fori_loop(0, blocks, block, 0)

    def finish(b, carry):
        both = jnp.concatenate([dkv[2 * b], dkv[2 * b + 1]], axis=0)
        out_ref[b, 2 * HD :, :] = both.T.astype(BF16)
        return carry

    lax.fori_loop(0, blocks, finish, 0)


def attend(tiles, valid, arrived):
    blocks, rows, tok = arrived.shape
    total = blocks * tok // TILE
    slots = 10 * TILE
    return pl.pallas_call(
        attend_body,
        in_specs=[
            pl.BlockSpec(memory_space=pltpu.SMEM),
            pl.BlockSpec(memory_space=pltpu.SMEM),
            pl.BlockSpec(memory_space=pltpu.VMEM),
        ],
        out_specs=pl.BlockSpec(memory_space=pltpu.VMEM),
        out_shape=jax.ShapeDtypeStruct(arrived.shape, BF16),
        scratch_shapes=[
            pltpu.VMEM((total, TILE, 2 * HD), BF16),
            pltpu.VMEM((total, 2 * HD, TILE), BF16),
            pltpu.VMEM((total, TILE, 2 * HD), F32),
        ],
        compiler_params=pltpu.CompilerParams(vmem_limit_bytes=48 * 2**20),
        cost_estimate=pl.CostEstimate(
            flops=blocks * 6 * 2 * tok * slots * HD,
            bytes_accessed=4 * 2**20,
            transcendentals=blocks * tok * slots,
        ),
        name="attend",
    )(tiles, valid, arrived)


def shards(inputs, cotangent, key_tiles, tile_valid, w_qkv, w_out):
    width = inputs.shape[2]
    x = inputs[0]
    cot = cotangent[0]
    myself = lax.axis_index("seq")
    sent = project(x, cot, w_qkv, w_out)
    arrived = lax.all_to_all(sent, "seq", split_axis=0, concat_axis=0, tiled=True)
    group_tiles = lax.dynamic_index_in_dim(key_tiles[0], myself // 4, 0, keepdims=False)
    results = attend(group_tiles, tile_valid[0], arrived)
    back = lax.all_to_all(results, "seq", split_axis=0, concat_axis=0, tiled=True)
    heads = jnp.stack([back[slot_of(h)] for h in range(H)], axis=0)
    tok = heads.shape[-1]
    heads = heads.reshape(H, 4, HD, tok).swapaxes(0, 1).reshape(4, width, tok)
    attended_t = heads[0]
    grad_proj_t = heads[1:].reshape(3 * width, tok)
    outputs = jnp.einsum("dt,de->te", attended_t, w_out, preferred_element_type=F32).astype(BF16)
    grad_inputs = jnp.einsum("et,de->td", grad_proj_t, w_qkv, preferred_element_type=F32).astype(
        BF16
    )
    first_part = jnp.einsum("td,et->de", x, grad_proj_t, preferred_element_type=F32)
    second_part = jnp.einsum("dt,te->de", attended_t, cot, preferred_element_type=F32)
    rows = width // 16
    whole = lax.psum(jnp.concatenate([first_part, second_part], axis=1), ("seq", "slide"))
    share = lax.dynamic_slice_in_dim(whole, myself * rows, rows, 0)
    return (outputs[None], grad_inputs[None], share[:, : 3 * width], share[:, 3 * width :])


def solution(mesh):
    placed = (
        P("slide", "seq", None),
        P("slide", "seq", None),
        P("slide", None, None, None),
        P("slide", None),
        P(),
        P(),
    )
    return jax.shard_map(
        shards,
        mesh=mesh,
        in_specs=placed,
        out_specs=(
            P("slide", "seq", None),
            P("slide", "seq", None),
            P("seq", None),
            P("seq", None),
        ),
        check_vma=False,
    )
```

```python
import jax
import jax.numpy as jnp
from jax import lax
from jax.experimental import pallas as pl
from jax.experimental.pallas import tpu as pltpu
from jax.sharding import PartitionSpec as P

H = 12
HPG = 3
HD = 64
TILE = 128
NEG_FILL = -1e30
F32 = jnp.float32
BF16 = jnp.bfloat16
SCALE = HD ** (-0.5)


def slot_of(head):
    row = head // HPG
    place = head % HPG
    return 4 * row + place + (place >= row)


def project_body(x_ref, cot_ref, wq_ref, wk_ref, wv_ref, wo_ref, out_ref):
    step = pl.program_id(0)
    x = x_ref[...]
    contract = (((0,), (1,)), ((), ()))
    qt = lax.dot_general(wq_ref[...], x, contract, preferred_element_type=F32).astype(BF16)
    kt = lax.dot_general(wk_ref[...], x, contract, preferred_element_type=F32).astype(BF16)
    vt = lax.dot_general(wv_ref[...], x, contract, preferred_element_type=F32).astype(BF16)
    gt = lax.dot_general(
        wo_ref[...], cot_ref[...], (((1,), (1,)), ((), ())), preferred_element_type=F32
    ).astype(BF16)
    qt = qt * jnp.asarray(SCALE, BF16)
    for half in range(2):
        head = 2 * step + half
        row = head // HPG
        place = head - row * HPG
        slot = 4 * row + place + jnp.where(place >= row, 1, 0)
        rows = slice(half * HD, half * HD + HD)
        out_ref[slot, 0:HD, :] = qt[rows]
        out_ref[slot, HD : 2 * HD, :] = kt[rows]
        out_ref[slot, 2 * HD : 3 * HD, :] = vt[rows]
        out_ref[slot, 3 * HD :, :] = gt[rows]

    @pl.when(step == 0)
    def _():
        for row in range(4):
            out_ref[5 * row] = jnp.zeros(out_ref.shape[1:], BF16)


def project(x, cot, w_qkv, w_out):
    tok, width = x.shape
    pairs = H // 2
    return pl.pallas_call(
        project_body,
        grid=(pairs,),
        in_specs=[
            pl.BlockSpec((tok, width), lambda i: (0, 0)),
            pl.BlockSpec((tok, width), lambda i: (0, 0)),
            pl.BlockSpec((width, 2 * HD), lambda i: (0, i)),
            pl.BlockSpec((width, 2 * HD), lambda i: (0, i + pairs)),
            pl.BlockSpec((width, 2 * HD), lambda i: (0, i + 2 * pairs)),
            pl.BlockSpec((2 * HD, width), lambda i: (i, 0)),
        ],
        out_specs=pl.BlockSpec((16, 4 * HD, tok), lambda i: (0, 0, 0)),
        out_shape=jax.ShapeDtypeStruct((16, 4 * HD, tok), BF16),
        compiler_params=pltpu.CompilerParams(vmem_limit_bytes=32 * 2**20),
        cost_estimate=pl.CostEstimate(
            flops=2 * tok * width * 4 * width, bytes_accessed=8 * 2**20, transcendentals=0
        ),
        name="project",
    )(x, cot, w_qkv, w_qkv, w_qkv, w_out)


def attend_body(tiles_ref, valid_ref, in_ref, out_ref, kv, kvt, dkv):
    blocks = in_ref.shape[0]
    listed = tiles_ref.shape[1]

    def prepare(b, carry):
        both = in_ref[b, HD : 3 * HD, :]
        flipped = both.T
        for c in range(2):
            kvt[2 * b + c] = both[:, c * TILE : (c + 1) * TILE]
            kv[2 * b + c] = flipped[c * TILE : (c + 1) * TILE]
            dkv[2 * b + c] = jnp.zeros((TILE, 2 * HD), F32)
        return carry

    lax.fori_loop(0, blocks, prepare, 0)

    def block(b, carry):
        tiles = [2 * b, 2 * b + 1] + [tiles_ref[b, i] for i in range(listed)]
        qt = in_ref[b, 0:HD, :]
        gt = in_ref[b, 3 * HD :, :]
        zero = jnp.zeros_like(qt)
        keys = jnp.concatenate([kv[t] for t in tiles], axis=0)
        scores = jnp.dot(
            keys, jnp.concatenate([qt, zero], axis=0), preferred_element_type=F32
        )
        grad_probs = jnp.dot(
            keys, jnp.concatenate([zero, gt], axis=0), preferred_element_type=F32
        )
        pieces = []
        for i, t in enumerate(tiles):
            bias = jnp.where(valid_ref[t] > 0, 0.0, NEG_FILL).astype(F32)
            pieces.append(scores[i * TILE : (i + 1) * TILE] + bias)
        scores = jnp.concatenate(pieces, axis=0)
        top = jnp.max(scores, axis=0, keepdims=True)
        expo = jnp.exp(scores - top)
        probs = expo * (1.0 / jnp.sum(expo, axis=0, keepdims=True))
        low = probs.astype(BF16)
        keys_t = jnp.concatenate([kvt[t, 0:HD] for t in tiles], axis=1)
        values_t = jnp.concatenate([kvt[t, HD:] for t in tiles], axis=1)
        attended = jnp.dot(values_t, low, preferred_element_type=F32)
        center = jnp.sum(attended * gt.astype(F32), axis=0, keepdims=True)
        grad_scores = (probs * (grad_probs - center)).astype(BF16)
        grad_q = jnp.dot(keys_t, grad_scores, preferred_element_type=F32) * SCALE
        out_ref[b, 0:HD, :] = attended.astype(BF16)
        out_ref[b, HD : 2 * HD, :] = grad_q.astype(BF16)
        flipped = jnp.concatenate([qt, gt], axis=0).T
        lane = lax.broadcasted_iota(jnp.int32, flipped.shape, 1)
        nothing = jnp.zeros_like(flipped)
        right = jnp.concatenate(
            [jnp.where(lane < HD, flipped, nothing), jnp.where(lane < HD, nothing, flipped)],
            axis=0,
        )
        terms = jnp.dot(
            jnp.concatenate([grad_scores, low], axis=1), right, preferred_element_type=F32
        )
        for i, t in enumerate(tiles):
            dkv[t] += terms[i * TILE : (i + 1) * TILE]
        return carry

    lax.fori_loop(0, blocks, block, 0)

    def finish(b, carry):
        both = jnp.concatenate([dkv[2 * b], dkv[2 * b + 1]], axis=0)
        out_ref[b, 2 * HD :, :] = both.T.astype(BF16)
        return carry

    lax.fori_loop(0, blocks, finish, 0)


def attend(tiles, valid, arrived):
    blocks, rows, tok = arrived.shape
    total = blocks * tok // TILE
    slots = 10 * TILE
    return pl.pallas_call(
        attend_body,
        in_specs=[
            pl.BlockSpec(memory_space=pltpu.SMEM),
            pl.BlockSpec(memory_space=pltpu.SMEM),
            pl.BlockSpec(memory_space=pltpu.VMEM),
        ],
        out_specs=pl.BlockSpec(memory_space=pltpu.VMEM),
        out_shape=jax.ShapeDtypeStruct(arrived.shape, BF16),
        scratch_shapes=[
            pltpu.VMEM((total, TILE, 2 * HD), BF16),
            pltpu.VMEM((total, 2 * HD, TILE), BF16),
            pltpu.VMEM((total, TILE, 2 * HD), F32),
        ],
        compiler_params=pltpu.CompilerParams(vmem_limit_bytes=48 * 2**20),
        cost_estimate=pl.CostEstimate(
            flops=blocks * 6 * 2 * tok * slots * HD,
            bytes_accessed=4 * 2**20,
            transcendentals=blocks * tok * slots,
        ),
        name="attend",
    )(tiles, valid, arrived)


def weigh_body(res_ref, x_ref, out_ref, acc):
    step = pl.program_id(0)
    part = jnp.dot(res_ref[0, HD:, :], x_ref[0], preferred_element_type=F32)

    @pl.when(step == 0)
    def _():
        acc[...] = part

    @pl.when(step > 0)
    def _():
        acc[...] += part

    @pl.when(step == pl.num_programs(0) - 1)
    def _():
        out_ref[...] = acc[...].T.astype(BF16)


def weigh(results, x_all):
    blocks, rows, tok = results.shape
    width = x_all.shape[2]
    wide = rows - HD
    return pl.pallas_call(
        weigh_body,
        grid=(blocks,),
        in_specs=[
            pl.BlockSpec((1, rows, tok), lambda i: (i, 0, 0)),
            pl.BlockSpec((1, tok, width), lambda i: (i, 0, 0)),
        ],
        out_specs=pl.BlockSpec((width, wide), lambda i: (0, 0)),
        out_shape=jax.ShapeDtypeStruct((width, wide), BF16),
        scratch_shapes=[pltpu.VMEM((wide, width), F32)],
        compiler_params=pltpu.CompilerParams(vmem_limit_bytes=32 * 2**20),
        cost_estimate=pl.CostEstimate(
            flops=2 * blocks * tok * width * wide,
            bytes_accessed=9 * 2**20,
            transcendentals=0,
        ),
        name="weigh",
    )(results, x_all)


def swap_cores(value):
    return lax.ppermute(value, "slide", [(i, i ^ 1) for i in range(lax.axis_size("slide"))])


def sum_slides(part):
    n = lax.axis_size("slide")
    core = lax.rem(lax.axis_index("slide"), 2)
    halves = part.reshape(2, part.shape[0] // 2, part.shape[1])
    mine = lax.dynamic_index_in_dim(halves, core, 0, keepdims=False)
    theirs = lax.dynamic_index_in_dim(halves, 1 - core, 0, keepdims=False)
    chip = (mine.astype(F32) + swap_cores(theirs).astype(F32)).astype(BF16)
    others = [
        lax.ppermute(chip, "slide", [(i, (i + 2 * k) % n) for i in range(n)]).astype(F32)
        for k in (1, 2, 3)
    ]
    total = (chip.astype(F32) + others[1]) + (others[0] + others[2])
    rest = swap_cores(total)
    return jnp.where(
        core == 0,
        jnp.concatenate([total, rest], axis=0),
        jnp.concatenate([rest, total], axis=0),
    )


def shards(inputs, cotangent, key_tiles, tile_valid, w_qkv, w_out):
    width = inputs.shape[2]
    x = inputs[0]
    cot = cotangent[0]
    tok = x.shape[0]
    peers = lax.axis_size("seq")
    myself = lax.axis_index("seq")
    x_all = lax.all_gather(x, "seq", axis=0)
    sent = project(x, cot, w_qkv, w_out)
    arrived = lax.all_to_all(sent, "seq", split_axis=0, concat_axis=0, tiled=True)
    group_tiles = lax.dynamic_index_in_dim(key_tiles[0], myself // 4, 0, keepdims=False)
    results = attend(group_tiles, tile_valid[0], arrived)
    back = lax.all_to_all(results, "seq", split_axis=0, concat_axis=0, tiled=True)
    heads = jnp.stack([back[slot_of(h)] for h in range(H)], axis=0)
    heads = heads.reshape(H, 4, HD, tok).swapaxes(0, 1).reshape(4, width, tok)
    attended_t = heads[0]
    grad_proj_t = heads[1:].reshape(3 * width, tok)
    outputs = jnp.einsum("dt,de->te", attended_t, w_out, preferred_element_type=F32).astype(BF16)
    grad_inputs = jnp.einsum("et,de->td", grad_proj_t, w_qkv, preferred_element_type=F32).astype(
        BF16
    )
    rows = width // peers
    in_part = weigh(results, x_all)
    out_part = jnp.einsum("dt,te->de", attended_t, cot, preferred_element_type=F32).astype(BF16)
    chunks = jnp.concatenate([in_part, out_part], axis=1).reshape(peers, rows, -1)
    spread = lax.all_to_all(chunks, "seq", split_axis=0, concat_axis=0, tiled=True)
    wide = 3 * HD
    in_rows = jnp.concatenate(
        [
            spread[slot_of(h), :, m * HD : (m + 1) * HD]
            for m in range(3)
            for h in range(H)
        ],
        axis=1,
    )
    out_rows = jnp.sum(spread[:, :, wide:].astype(F32), axis=0).astype(BF16)
    total = sum_slides(jnp.concatenate([in_rows, out_rows], axis=1))
    return (outputs[None], grad_inputs[None], total[:, : 3 * width], total[:, 3 * width :])


def solution(mesh):
    placed = (
        P("slide", "seq", None),
        P("slide", "seq", None),
        P("slide", None, None, None),
        P("slide", None),
        P(),
        P(),
    )
    return jax.shard_map(
        shards,
        mesh=mesh,
        in_specs=placed,
        out_specs=(
            P("slide", "seq", None),
            P("slide", "seq", None),
            P("seq", None),
            P("seq", None),
        ),
        check_vma=False,
    )
```

```python
import jax
import jax.numpy as jnp
from jax import lax
from jax.experimental import pallas as pl
from jax.experimental.pallas import tpu as pltpu
from jax.sharding import PartitionSpec as P

H = 12
HPG = 3
HD = 64
TILE = 128
NEG_FILL = -1e30
F32 = jnp.float32
BF16 = jnp.bfloat16
SCALE = HD ** (-0.5)
NB = 4


def slot_of(head):
    row = head // HPG
    place = head % HPG
    return 4 * row + place + (place >= row)


def project_body(x_ref, cot_ref, wq_ref, wk_ref, wv_ref, wo_ref, out_ref):
    step = pl.program_id(0)
    x = x_ref[...]
    contract = (((0,), (1,)), ((), ()))
    qt = lax.dot_general(wq_ref[...], x, contract, preferred_element_type=F32).astype(BF16)
    kt = lax.dot_general(wk_ref[...], x, contract, preferred_element_type=F32).astype(BF16)
    vt = lax.dot_general(wv_ref[...], x, contract, preferred_element_type=F32).astype(BF16)
    gt = lax.dot_general(
        wo_ref[...], cot_ref[...], (((1,), (1,)), ((), ())), preferred_element_type=F32
    ).astype(BF16)
    qt = qt * jnp.asarray(SCALE, BF16)
    for half in range(2):
        head = 2 * step + half
        row = head // HPG
        place = head - row * HPG
        slot = 4 * row + place + jnp.where(place >= row, 1, 0)
        rows = slice(half * HD, half * HD + HD)
        out_ref[slot, 0:HD, :] = qt[rows]
        out_ref[slot, HD : 2 * HD, :] = kt[rows]
        out_ref[slot, 2 * HD : 3 * HD, :] = vt[rows]
        out_ref[slot, 3 * HD :, :] = gt[rows]

    @pl.when(step == 0)
    def _():
        for row in range(4):
            out_ref[5 * row] = jnp.zeros(out_ref.shape[1:], BF16)


def project(x, cot, w_qkv, w_out):
    tok, width = x.shape
    pairs = H // 2
    return pl.pallas_call(
        project_body,
        grid=(pairs,),
        in_specs=[
            pl.BlockSpec((tok, width), lambda i: (0, 0)),
            pl.BlockSpec((tok, width), lambda i: (0, 0)),
            pl.BlockSpec((width, 2 * HD), lambda i: (0, i)),
            pl.BlockSpec((width, 2 * HD), lambda i: (0, i + pairs)),
            pl.BlockSpec((width, 2 * HD), lambda i: (0, i + 2 * pairs)),
            pl.BlockSpec((2 * HD, width), lambda i: (i, 0)),
        ],
        out_specs=pl.BlockSpec((16, 4 * HD, tok), lambda i: (0, 0, 0)),
        out_shape=jax.ShapeDtypeStruct((16, 4 * HD, tok), BF16),
        compiler_params=pltpu.CompilerParams(vmem_limit_bytes=32 * 2**20),
        cost_estimate=pl.CostEstimate(
            flops=2 * tok * width * 4 * width, bytes_accessed=8 * 2**20, transcendentals=0
        ),
        name="project",
    )(x, cot, w_qkv, w_qkv, w_qkv, w_out)


def forward_body(tiles_ref, valid_ref, in_ref, att_ref, exp_ref, stat_ref, kv, vt):
    b = pl.program_id(0)
    blocks = in_ref.shape[0]
    listed = tiles_ref.shape[1]

    @pl.when(b == 0)
    def _():
        def prepare(i, carry):
            both = in_ref[i, HD : 3 * HD, :]
            flipped = both.T
            for c in range(2):
                vt[2 * i + c] = both[HD:, c * TILE : (c + 1) * TILE]
                kv[2 * i + c] = flipped[c * TILE : (c + 1) * TILE]
            return carry

        lax.fori_loop(0, blocks, prepare, 0)

    work = []
    for n in range(NB):
        p = NB * b + n
        tiles = [2 * p, 2 * p + 1] + [tiles_ref[p, i] for i in range(listed)]
        qt = in_ref[p, 0:HD, :]
        keys = jnp.concatenate([kv[t] for t in tiles], axis=0)
        scores = jnp.dot(
            keys, jnp.concatenate([qt, jnp.zeros_like(qt)], axis=0), preferred_element_type=F32
        )
        work.append((n, p, tiles, scores))
    for n, p, tiles, scores in work:
        gt = in_ref[p, 3 * HD :, :]
        pieces = []
        for i, t in enumerate(tiles):
            bias = jnp.where(valid_ref[t] > 0, 0.0, NEG_FILL).astype(F32)
            pieces.append(scores[i * TILE : (i + 1) * TILE] + bias)
        scores = jnp.concatenate(pieces, axis=0)
        top = jnp.max(scores, axis=0, keepdims=True)
        expo = jnp.exp(scores - top)
        share = 1.0 / jnp.sum(expo, axis=0, keepdims=True)
        low = expo.astype(BF16)
        exp_ref[n] = low
        values_t = jnp.concatenate([vt[t] for t in tiles], axis=1)
        attended = jnp.dot(values_t, low, preferred_element_type=F32) * share
        scaled = (gt.astype(F32) * share).astype(BF16)
        center = jnp.sum(attended * scaled.astype(F32), axis=0, keepdims=True)
        att_ref[p] = attended.astype(BF16)
        stat_ref[p, 0:1, :] = share
        stat_ref[p, 1:2, :] = center


def forward(tiles, valid, arrived):
    blocks, rows, tok = arrived.shape
    total = blocks * tok // TILE
    slots = 10 * TILE
    whole = pl.BlockSpec(memory_space=pltpu.VMEM)
    return pl.pallas_call(
        forward_body,
        grid=(blocks // NB,),
        in_specs=[
            pl.BlockSpec(memory_space=pltpu.SMEM),
            pl.BlockSpec(memory_space=pltpu.SMEM),
            whole,
        ],
        out_specs=[whole, pl.BlockSpec((NB, slots, tok), lambda i: (i, 0, 0)), whole],
        out_shape=[
            jax.ShapeDtypeStruct((blocks, HD, tok), BF16),
            jax.ShapeDtypeStruct((blocks, slots, tok), BF16),
            jax.ShapeDtypeStruct((blocks, 8, tok), F32),
        ],
        scratch_shapes=[
            pltpu.VMEM((total, TILE, 2 * HD), BF16),
            pltpu.VMEM((total, HD, TILE), BF16),
        ],
        compiler_params=pltpu.CompilerParams(vmem_limit_bytes=60 * 2**20),
        cost_estimate=pl.CostEstimate(
            flops=blocks * 4 * 2 * tok * slots * 2 * HD,
            bytes_accessed=14 * 2**20,
            transcendentals=blocks * tok * slots,
        ),
        name="forward",
    )(tiles, valid, arrived)


def backward_body(tiles_ref, in_ref, exp_ref, stat_ref, out_ref, kv, kt, dkv):
    b = pl.program_id(0)
    blocks = in_ref.shape[0]
    listed = tiles_ref.shape[1]

    @pl.when(b == 0)
    def _():
        def prepare(i, carry):
            both = in_ref[i, HD : 3 * HD, :]
            flipped = both.T
            for c in range(2):
                kt[2 * i + c] = both[:HD, c * TILE : (c + 1) * TILE]
                kv[2 * i + c] = flipped[c * TILE : (c + 1) * TILE]
                dkv[2 * i + c] = jnp.zeros((TILE, 2 * HD), F32)
            return carry

        lax.fori_loop(0, blocks, prepare, 0)

    work = []
    for n in range(NB):
        p = NB * b + n
        tiles = [2 * p, 2 * p + 1] + [tiles_ref[p, i] for i in range(listed)]
        gt = in_ref[p, 3 * HD :, :]
        scaled = (gt.astype(F32) * stat_ref[p, 0:1, :]).astype(BF16)
        keys = jnp.concatenate([kv[t] for t in tiles], axis=0)
        grad_probs = jnp.dot(
            keys,
            jnp.concatenate([jnp.zeros_like(scaled), scaled], axis=0),
            preferred_element_type=F32,
        )
        work.append((n, p, tiles, scaled, grad_probs))
    for n, p, tiles, scaled, grad_probs in work:
        qt = in_ref[p, 0:HD, :]
        low = exp_ref[n]
        center = stat_ref[p, 1:2, :]
        grad_scores = (low.astype(F32) * (grad_probs - center)).astype(BF16)
        keys_t = jnp.concatenate([kt[t] for t in tiles], axis=1)
        grad_q = jnp.dot(keys_t, grad_scores, preferred_element_type=F32) * SCALE
        out_ref[p, 0:HD, :] = grad_q.astype(BF16)
        flipped = jnp.concatenate([qt, scaled], axis=0).T
        lane = lax.broadcasted_iota(jnp.int32, flipped.shape, 1)
        nothing = jnp.zeros_like(flipped)
        right = jnp.concatenate(
            [jnp.where(lane < HD, flipped, nothing), jnp.where(lane < HD, nothing, flipped)],
            axis=0,
        )
        terms = jnp.dot(
            jnp.concatenate([grad_scores, low], axis=1), right, preferred_element_type=F32
        )
        for i, t in enumerate(tiles):
            dkv[t] += terms[i * TILE : (i + 1) * TILE]

    @pl.when(b == blocks // NB - 1)
    def _():
        def finish(i, carry):
            both = jnp.concatenate([dkv[2 * i], dkv[2 * i + 1]], axis=0)
            out_ref[i, HD:, :] = both.T.astype(BF16)
            return carry

        lax.fori_loop(0, blocks, finish, 0)


def backward(tiles, arrived, low, stats):
    blocks, rows, tok = arrived.shape
    total = blocks * tok // TILE
    slots = 10 * TILE
    whole = pl.BlockSpec(memory_space=pltpu.VMEM)
    return pl.pallas_call(
        backward_body,
        grid=(blocks // NB,),
        in_specs=[
            pl.BlockSpec(memory_space=pltpu.SMEM),
            whole,
            pl.BlockSpec((NB, slots, tok), lambda i: (i, 0, 0)),
            whole,
        ],
        out_specs=whole,
        out_shape=jax.ShapeDtypeStruct((blocks, 3 * HD, tok), BF16),
        scratch_shapes=[
            pltpu.VMEM((total, TILE, 2 * HD), BF16),
            pltpu.VMEM((total, HD, TILE), BF16),
            pltpu.VMEM((total, TILE, 2 * HD), F32),
        ],
        compiler_params=pltpu.CompilerParams(vmem_limit_bytes=60 * 2**20),
        cost_estimate=pl.CostEstimate(
            flops=blocks * 8 * 2 * tok * slots * 2 * HD,
            bytes_accessed=16 * 2**20,
            transcendentals=0,
        ),
        name="backward",
    )(tiles, arrived, low, stats)


def weigh_body(res_ref, x_ref, back_ref, cot_ref, w_ref, chunk_ref, out_ref, acc):
    step = pl.program_id(0)
    part = jnp.dot(res_ref[0], x_ref[0], preferred_element_type=F32)

    @pl.when(step == 0)
    def _():
        attended = jnp.concatenate([back_ref[slot_of(h)] for h in range(H)], axis=0)
        chunk_ref[:, : cot_ref.shape[1]] = jnp.dot(
            attended, cot_ref[...], preferred_element_type=F32
        ).astype(BF16)
        out_ref[...] = jnp.dot(attended.T, w_ref[...], preferred_element_type=F32).astype(BF16)
        acc[...] = part

    @pl.when(step > 0)
    def _():
        acc[...] += part

    @pl.when(step == pl.num_programs(0) - 1)
    def _():
        chunk_ref[:, cot_ref.shape[1] :] = acc[...].T.astype(BF16)


def weigh(results, x_all, att_back, cot, w_out):
    blocks, wide, tok = results.shape
    width = x_all.shape[2]
    whole = pl.BlockSpec(memory_space=pltpu.VMEM)
    return pl.pallas_call(
        weigh_body,
        grid=(blocks,),
        in_specs=[
            pl.BlockSpec((1, wide, tok), lambda i: (i, 0, 0)),
            pl.BlockSpec((1, tok, width), lambda i: (i, 0, 0)),
            whole,
            whole,
            whole,
        ],
        out_specs=[whole, whole],
        out_shape=[
            jax.ShapeDtypeStruct((width, width + wide), BF16),
            jax.ShapeDtypeStruct((tok, width), BF16),
        ],
        scratch_shapes=[pltpu.VMEM((wide, width), F32)],
        compiler_params=pltpu.CompilerParams(vmem_limit_bytes=60 * 2**20),
        cost_estimate=pl.CostEstimate(
            flops=2 * blocks * tok * width * wide,
            bytes_accessed=10 * 2**20,
            transcendentals=0,
        ),
        name="weigh",
    )(results, x_all, att_back, cot, w_out)


def collect_body(core_ref, spread_ref, mine_ref, theirs_ref):
    width = spread_ref.shape[2] - 3 * HD
    out_rows = spread_ref[0, :, :width].astype(F32)
    for source in range(1, spread_ref.shape[0]):
        out_rows += spread_ref[source, :, :width].astype(F32)
    parts = [
        jnp.concatenate(
            [
                spread_ref[slot_of(h), :, width + m * HD : width + (m + 1) * HD]
                for h in range(H)
            ],
            axis=1,
        )
        for m in range(3)
    ]
    low = jnp.concatenate(parts[:2], axis=1)
    high = jnp.concatenate([parts[2], out_rows.astype(BF16)], axis=1)

    @pl.when(core_ref[0] == 0)
    def _():
        mine_ref[...] = low
        theirs_ref[...] = high

    @pl.when(core_ref[0] != 0)
    def _():
        mine_ref[...] = high
        theirs_ref[...] = low


def collect(core, spread):
    peers, rows, wide = spread.shape
    half = 2 * (wide - 3 * HD)
    whole = pl.BlockSpec(memory_space=pltpu.VMEM)
    return pl.pallas_call(
        collect_body,
        in_specs=[pl.BlockSpec(memory_space=pltpu.SMEM), whole],
        out_specs=[whole, whole],
        out_shape=[jax.ShapeDtypeStruct((rows, half), BF16)] * 2,
        compiler_params=pltpu.CompilerParams(vmem_limit_bytes=16 * 2**20),
        cost_estimate=pl.CostEstimate(flops=10**6, bytes_accessed=2 * 10**6, transcendentals=0),
        name="collect",
    )(core, spread)


def close_body(back_ref, w_ref, out_ref):
    grad = jnp.concatenate(
        [
            back_ref[slot_of(h), m * HD : (m + 1) * HD, :]
            for m in range(3)
            for h in range(H)
        ],
        axis=0,
    )
    out_ref[...] = lax.dot_general(
        grad.T, w_ref[...], (((1,), (1,)), ((), ())), preferred_element_type=F32
    ).astype(BF16)


def close(back, w_qkv):
    tok = back.shape[2]
    width = w_qkv.shape[0]
    whole = pl.BlockSpec(memory_space=pltpu.VMEM)
    return pl.pallas_call(
        close_body,
        in_specs=[whole, whole],
        out_specs=whole,
        out_shape=jax.ShapeDtypeStruct((tok, width), BF16),
        compiler_params=pltpu.CompilerParams(vmem_limit_bytes=32 * 2**20),
        cost_estimate=pl.CostEstimate(
            flops=2 * tok * width * 3 * width, bytes_accessed=6 * 2**20, transcendentals=0
        ),
        name="close",
    )(back, w_qkv)


def swap_cores(value):
    return lax.ppermute(value, "slide", [(i, i ^ 1) for i in range(lax.axis_size("slide"))])


def sum_slides(core, mine, theirs):
    n = lax.axis_size("slide")
    chip = (mine.astype(F32) + swap_cores(theirs).astype(F32)).astype(BF16)
    others = [
        lax.ppermute(chip, "slide", [(i, (i + 2 * k) % n) for i in range(n)]).astype(F32)
        for k in (1, 2, 3)
    ]
    total = (chip.astype(F32) + others[1]) + (others[0] + others[2])
    rest = swap_cores(total)
    return jnp.where(core == 0, total, rest), jnp.where(core == 0, rest, total)


def shards(inputs, cotangent, key_tiles, tile_valid, w_qkv, w_out):
    width = inputs.shape[2]
    x = inputs[0]
    cot = cotangent[0]
    peers = lax.axis_size("seq")
    myself = lax.axis_index("seq")
    core = lax.rem(lax.axis_index("slide"), 2)
    x_all = lax.all_gather(x, "seq", axis=0)
    sent = project(x, cot, w_qkv, w_out)
    arrived = lax.all_to_all(sent, "seq", split_axis=0, concat_axis=0, tiled=True)
    group_tiles = lax.dynamic_index_in_dim(key_tiles[0], myself // 4, 0, keepdims=False)
    att_sent, low, stats = forward(group_tiles, tile_valid[0], arrived)
    att_back = lax.all_to_all(att_sent, "seq", split_axis=0, concat_axis=0, tiled=True)
    results = backward(group_tiles, arrived, low, stats)
    chunks, outputs = weigh(results, x_all, att_back, cot, w_out)
    chunks = chunks.reshape(peers, width // peers, -1)
    spread = lax.all_to_all(chunks, "seq", split_axis=0, concat_axis=0, tiled=True)
    results, spread = lax.optimization_barrier((results, spread))
    back = lax.all_to_all(results, "seq", split_axis=0, concat_axis=0, tiled=True)
    mine, theirs = collect(core[None], spread)
    low_half, high_half = sum_slides(core, mine, theirs)
    grad_inputs = close(back, w_qkv)
    return (
        outputs[None],
        grad_inputs[None],
        jnp.concatenate([low_half, high_half[:, :width]], axis=1),
        high_half[:, width:],
    )


def solution(mesh):
    placed = (
        P("slide", "seq", None),
        P("slide", "seq", None),
        P("slide", None, None, None),
        P("slide", None),
        P(),
        P(),
    )
    return jax.shard_map(
        shards,
        mesh=mesh,
        in_specs=placed,
        out_specs=(
            P("slide", "seq", None),
            P("slide", "seq", None),
            P("seq", None),
            P("seq", None),
        ),
        check_vma=False,
    )
```

```python
import jax
import jax.numpy as jnp
from jax import lax
from jax.experimental import pallas as pl
from jax.experimental.pallas import tpu as pltpu
from jax.sharding import PartitionSpec as P

H = 12
HPG = 3
HD = 64
TILE = 128
NEG_FILL = -1e30
F32 = jnp.float32
BF16 = jnp.bfloat16
SCALE = HD ** (-0.5)
NB = 4


def slot_of(head):
    row = head // HPG
    place = head % HPG
    return 4 * row + place + (place >= row)


def project_body(x_ref, cot_ref, wq_ref, wk_ref, wv_ref, wo_ref, out_ref):
    step = pl.program_id(0)
    x = x_ref[...]
    qt, kt, vt = [
        jnp.dot(x, ref[...], preferred_element_type=F32).astype(BF16).T
        for ref in (wq_ref, wk_ref, wv_ref)
    ]
    gt = lax.dot_general(
        wo_ref[...], cot_ref[...], (((1,), (1,)), ((), ())), preferred_element_type=F32
    ).astype(BF16)
    qt = qt * jnp.asarray(SCALE, BF16)
    for half in range(2):
        head = 2 * step + half
        row = head // HPG
        place = head - row * HPG
        slot = 4 * row + place + jnp.where(place >= row, 1, 0)
        rows = slice(half * HD, half * HD + HD)
        out_ref[slot, 0:HD, :] = qt[rows]
        out_ref[slot, HD : 2 * HD, :] = kt[rows]
        out_ref[slot, 2 * HD : 3 * HD, :] = vt[rows]
        out_ref[slot, 3 * HD :, :] = gt[rows]

    @pl.when(step == 0)
    def _():
        for row in range(4):
            out_ref[5 * row] = jnp.zeros(out_ref.shape[1:], BF16)


def project(x, cot, w_qkv, w_out):
    tok, width = x.shape
    pairs = H // 2
    return pl.pallas_call(
        project_body,
        grid=(pairs,),
        in_specs=[
            pl.BlockSpec((tok, width), lambda i: (0, 0)),
            pl.BlockSpec((tok, width), lambda i: (0, 0)),
            pl.BlockSpec((width, 2 * HD), lambda i: (0, i)),
            pl.BlockSpec((width, 2 * HD), lambda i: (0, i + pairs)),
            pl.BlockSpec((width, 2 * HD), lambda i: (0, i + 2 * pairs)),
            pl.BlockSpec((2 * HD, width), lambda i: (i, 0)),
        ],
        out_specs=pl.BlockSpec((16, 4 * HD, tok), lambda i: (0, 0, 0)),
        out_shape=jax.ShapeDtypeStruct((16, 4 * HD, tok), BF16),
        compiler_params=pltpu.CompilerParams(vmem_limit_bytes=60 * 2**20),
        cost_estimate=pl.CostEstimate(
            flops=2 * tok * width * 4 * width, bytes_accessed=8 * 2**20, transcendentals=0
        ),
        name="project",
    )(x, cot, w_qkv, w_qkv, w_qkv, w_out)


def forward_body(tiles_ref, valid_ref, in_ref, att_ref, exp_ref, stat_ref, kv, vt):
    b = pl.program_id(0)
    blocks = in_ref.shape[0]
    listed = tiles_ref.shape[1]

    @pl.when(b == 0)
    def _():
        def prepare(i, carry):
            both = in_ref[i, HD : 3 * HD, :]
            flipped = both.T
            for c in range(2):
                vt[2 * i + c] = both[HD:, c * TILE : (c + 1) * TILE]
                kv[2 * i + c] = flipped[c * TILE : (c + 1) * TILE]
            return carry

        lax.fori_loop(0, blocks, prepare, 0)

    work = []
    for n in range(NB):
        p = NB * b + n
        tiles = [2 * p, 2 * p + 1] + [tiles_ref[p, i] for i in range(listed)]
        qt = in_ref[p, 0:HD, :]
        keys = jnp.concatenate([kv[t] for t in tiles], axis=0)
        scores = jnp.dot(
            keys, jnp.concatenate([qt, jnp.zeros_like(qt)], axis=0), preferred_element_type=F32
        )
        work.append((n, p, tiles, scores))
    for n, p, tiles, scores in work:
        gt = in_ref[p, 3 * HD :, :]
        pieces = []
        for i, t in enumerate(tiles):
            bias = jnp.where(valid_ref[t] > 0, 0.0, NEG_FILL).astype(F32)
            pieces.append(scores[i * TILE : (i + 1) * TILE] + bias)
        scores = jnp.concatenate(pieces, axis=0)
        top = jnp.max(scores, axis=0, keepdims=True)
        expo = jnp.exp(scores - top)
        share = 1.0 / jnp.sum(expo, axis=0, keepdims=True)
        low = expo.astype(BF16)
        exp_ref[n] = low
        values_t = jnp.concatenate([vt[t] for t in tiles], axis=1)
        attended = jnp.dot(values_t, low, preferred_element_type=F32) * share
        scaled = (gt.astype(F32) * share).astype(BF16)
        center = jnp.sum(attended * scaled.astype(F32), axis=0, keepdims=True)
        att_ref[p] = attended.astype(BF16)
        stat_ref[p, 0:1, :] = share
        stat_ref[p, 1:2, :] = center


def forward(tiles, valid, arrived):
    blocks, rows, tok = arrived.shape
    total = blocks * tok // TILE
    slots = 10 * TILE
    whole = pl.BlockSpec(memory_space=pltpu.VMEM)
    return pl.pallas_call(
        forward_body,
        grid=(blocks // NB,),
        in_specs=[
            pl.BlockSpec(memory_space=pltpu.SMEM),
            pl.BlockSpec(memory_space=pltpu.SMEM),
            whole,
        ],
        out_specs=[whole, pl.BlockSpec((NB, slots, tok), lambda i: (i, 0, 0)), whole],
        out_shape=[
            jax.ShapeDtypeStruct((blocks, HD, tok), BF16),
            jax.ShapeDtypeStruct((blocks, slots, tok), BF16),
            jax.ShapeDtypeStruct((blocks, 8, tok), F32),
        ],
        scratch_shapes=[
            pltpu.VMEM((total, TILE, 2 * HD), BF16),
            pltpu.VMEM((total, HD, TILE), BF16),
        ],
        compiler_params=pltpu.CompilerParams(vmem_limit_bytes=60 * 2**20),
        cost_estimate=pl.CostEstimate(
            flops=blocks * 4 * 2 * tok * slots * 2 * HD,
            bytes_accessed=14 * 2**20,
            transcendentals=blocks * tok * slots,
        ),
        name="forward",
    )(tiles, valid, arrived)


def backward_body(tiles_ref, in_ref, exp_ref, stat_ref, out_ref, kv, kt, dkv):
    b = pl.program_id(0)
    blocks = in_ref.shape[0]
    listed = tiles_ref.shape[1]

    @pl.when(b == 0)
    def _():
        def prepare(i, carry):
            both = in_ref[i, HD : 3 * HD, :]
            flipped = both.T
            for c in range(2):
                kt[2 * i + c] = both[:HD, c * TILE : (c + 1) * TILE]
                kv[2 * i + c] = flipped[c * TILE : (c + 1) * TILE]
                dkv[2 * i + c] = jnp.zeros((TILE, 2 * HD), F32)
            return carry

        lax.fori_loop(0, blocks, prepare, 0)

    work = []
    for n in range(NB):
        p = NB * b + n
        tiles = [2 * p, 2 * p + 1] + [tiles_ref[p, i] for i in range(listed)]
        gt = in_ref[p, 3 * HD :, :]
        scaled = (gt.astype(F32) * stat_ref[p, 0:1, :]).astype(BF16)
        keys = jnp.concatenate([kv[t] for t in tiles], axis=0)
        grad_probs = jnp.dot(
            keys,
            jnp.concatenate([jnp.zeros_like(scaled), scaled], axis=0),
            preferred_element_type=F32,
        )
        work.append((n, p, tiles, scaled, grad_probs))
    for n, p, tiles, scaled, grad_probs in work:
        qt = in_ref[p, 0:HD, :]
        low = exp_ref[n]
        center = stat_ref[p, 1:2, :]
        grad_scores = (low.astype(F32) * (grad_probs - center)).astype(BF16)
        keys_t = jnp.concatenate([kt[t] for t in tiles], axis=1)
        grad_q = jnp.dot(keys_t, grad_scores, preferred_element_type=F32) * SCALE
        out_ref[p, 0:HD, :] = grad_q.astype(BF16)
        flipped = jnp.concatenate([qt, scaled], axis=0).T
        lane = lax.broadcasted_iota(jnp.int32, flipped.shape, 1)
        nothing = jnp.zeros_like(flipped)
        right = jnp.concatenate(
            [jnp.where(lane < HD, flipped, nothing), jnp.where(lane < HD, nothing, flipped)],
            axis=0,
        )
        terms = jnp.dot(
            jnp.concatenate([grad_scores, low], axis=1), right, preferred_element_type=F32
        )
        for i, t in enumerate(tiles):
            dkv[t] += terms[i * TILE : (i + 1) * TILE]

    @pl.when(b == blocks // NB - 1)
    def _():
        def finish(i, carry):
            both = jnp.concatenate([dkv[2 * i], dkv[2 * i + 1]], axis=0)
            out_ref[i, HD:, :] = both.T.astype(BF16)
            return carry

        lax.fori_loop(0, blocks, finish, 0)


def backward(tiles, arrived, low, stats):
    blocks, rows, tok = arrived.shape
    total = blocks * tok // TILE
    slots = 10 * TILE
    whole = pl.BlockSpec(memory_space=pltpu.VMEM)
    return pl.pallas_call(
        backward_body,
        grid=(blocks // NB,),
        in_specs=[
            pl.BlockSpec(memory_space=pltpu.SMEM),
            whole,
            pl.BlockSpec((NB, slots, tok), lambda i: (i, 0, 0)),
            whole,
        ],
        out_specs=whole,
        out_shape=jax.ShapeDtypeStruct((blocks, 3 * HD, tok), BF16),
        scratch_shapes=[
            pltpu.VMEM((total, TILE, 2 * HD), BF16),
            pltpu.VMEM((total, HD, TILE), BF16),
            pltpu.VMEM((total, TILE, 2 * HD), F32),
        ],
        compiler_params=pltpu.CompilerParams(vmem_limit_bytes=60 * 2**20),
        cost_estimate=pl.CostEstimate(
            flops=blocks * 8 * 2 * tok * slots * 2 * HD,
            bytes_accessed=16 * 2**20,
            transcendentals=0,
        ),
        name="backward",
    )(tiles, arrived, low, stats)


def weigh_body(core_ref, res_ref, x_ref, back_ref, cot_ref, mine_ref, theirs_ref, acc, out_acc):
    step = pl.program_id(0)
    part = jnp.dot(res_ref[0], x_ref[0], preferred_element_type=F32)
    for i in range(1, res_ref.shape[0]):
        part += jnp.dot(res_ref[i], x_ref[i], preferred_element_type=F32)

    @pl.when(step == 0)
    def _():
        attended = jnp.concatenate([back_ref[slot_of(h)] for h in range(H)], axis=0)
        out_acc[...] = jnp.dot(attended, cot_ref[...], preferred_element_type=F32).astype(BF16)
        acc[...] = part

    @pl.when(step > 0)
    def _():
        acc[...] += part

    @pl.when(step == pl.num_programs(0) - 1)
    def _():
        in_part = acc[...].T.astype(BF16)
        out_part = out_acc[...]
        rows, width = out_part.shape
        out_cols = width // 8
        in_cols = in_part.shape[1] // 8
        fill = jnp.zeros((rows, 128 - out_cols - in_cols), BF16)
        pieces = [
            jnp.concatenate(
                [
                    out_part[:, k * out_cols : (k + 1) * out_cols],
                    in_part[:, k * in_cols : (k + 1) * in_cols],
                    fill,
                ],
                axis=1,
            )
            for k in range(8)
        ]

        @pl.when(core_ref[0] == 0)
        def _():
            for k in range(4):
                mine_ref[k] = pieces[2 * k]
                theirs_ref[k] = pieces[2 * k + 1]

        @pl.when(core_ref[0] != 0)
        def _():
            for k in range(4):
                mine_ref[k] = pieces[2 * k + 1]
                theirs_ref[k] = pieces[2 * k]


def weigh(core, results, x_all, att_back, cot):
    blocks, wide, tok = results.shape
    width = x_all.shape[2]
    whole = pl.BlockSpec(memory_space=pltpu.VMEM)
    return pl.pallas_call(
        weigh_body,
        grid=(blocks // 4,),
        in_specs=[
            pl.BlockSpec(memory_space=pltpu.SMEM),
            pl.BlockSpec((4, wide, tok), lambda i: (i, 0, 0)),
            pl.BlockSpec((4, tok, width), lambda i: (i, 0, 0)),
            whole,
            whole,
        ],
        out_specs=[whole, whole],
        out_shape=[jax.ShapeDtypeStruct((4, width, 128), BF16)] * 2,
        scratch_shapes=[pltpu.VMEM((wide, width), F32), pltpu.VMEM((width, width), BF16)],
        compiler_params=pltpu.CompilerParams(vmem_limit_bytes=60 * 2**20),
        cost_estimate=pl.CostEstimate(
            flops=2 * blocks * tok * width * wide,
            bytes_accessed=10 * 2**20,
            transcendentals=0,
        ),
        name="weigh",
    )(core, results, x_all, att_back, cot)


def merge_body(chip_ref, mine_ref, got_ref, *outs):
    for k, out in enumerate(outs):
        place = lax.rem(chip_ref[0] + k, 4)
        out[...] = (mine_ref[place].astype(F32) + got_ref[place].astype(F32)).astype(BF16)


def merge(chip, mine, got):
    whole = pl.BlockSpec(memory_space=pltpu.VMEM)
    return pl.pallas_call(
        merge_body,
        in_specs=[pl.BlockSpec(memory_space=pltpu.SMEM), whole, whole],
        out_specs=[whole] * 4,
        out_shape=[jax.ShapeDtypeStruct(mine.shape[1:], BF16)] * 4,
        compiler_params=pltpu.CompilerParams(vmem_limit_bytes=16 * 2**20),
        cost_estimate=pl.CostEstimate(flops=10**6, bytes_accessed=2 * 10**6, transcendentals=0),
        name="merge",
    )(chip, mine, got)


def collect_body(spread_ref, out_ref):
    in_cols = 3 * HD // 8
    out_cols = 4 * in_cols
    total = spread_ref[0].astype(F32)
    for source in range(1, spread_ref.shape[0]):
        total += spread_ref[source].astype(F32)
    ins = [spread_ref[slot_of(h), :, out_cols : out_cols + in_cols].astype(F32) for h in range(H)]
    out_ref[...] = jnp.concatenate([total[:, :out_cols]] + ins, axis=1).astype(BF16)


def collect(spread):
    whole = pl.BlockSpec(memory_space=pltpu.VMEM)
    rows = spread.shape[1]
    return pl.pallas_call(
        collect_body,
        in_specs=[whole],
        out_specs=whole,
        out_shape=jax.ShapeDtypeStruct((rows, 6 * HD), BF16),
        compiler_params=pltpu.CompilerParams(vmem_limit_bytes=16 * 2**20),
        cost_estimate=pl.CostEstimate(flops=10**6, bytes_accessed=10**6, transcendentals=0),
        name="collect",
    )(spread)


def settle_body(all_ref, in_ref, out_ref):
    in_cols = 3 * HD // 8
    out_cols = 4 * in_cols
    parts = [all_ref[k].astype(F32) for k in range(8)]
    out_ref[...] = jnp.concatenate([part[:, :out_cols] for part in parts], axis=1)
    heads = [
        jnp.concatenate(
            [part[:, out_cols + h * in_cols : out_cols + (h + 1) * in_cols] for part in parts],
            axis=1,
        )
        for h in range(H)
    ]
    in_ref[...] = jnp.concatenate(
        [head[:, m * HD : (m + 1) * HD] for m in range(3) for head in heads], axis=1
    )


def settle(gathered):
    whole = pl.BlockSpec(memory_space=pltpu.VMEM)
    rows = gathered.shape[1]
    width = H * HD
    return pl.pallas_call(
        settle_body,
        in_specs=[whole],
        out_specs=[whole, whole],
        out_shape=[
            jax.ShapeDtypeStruct((rows, 3 * width), F32),
            jax.ShapeDtypeStruct((rows, width), F32),
        ],
        compiler_params=pltpu.CompilerParams(vmem_limit_bytes=16 * 2**20),
        cost_estimate=pl.CostEstimate(flops=10**6, bytes_accessed=10**6, transcendentals=0),
        name="settle",
    )(gathered)


def close_body(back_ref, att_ref, w_ref, wo_ref, grad_ref, out_ref):
    grad = jnp.concatenate(
        [
            back_ref[slot_of(h), m * HD : (m + 1) * HD, :]
            for m in range(3)
            for h in range(H)
        ],
        axis=0,
    )
    grad_ref[...] = lax.dot_general(
        grad.T, w_ref[...], (((1,), (1,)), ((), ())), preferred_element_type=F32
    ).astype(BF16)
    attended = jnp.concatenate([att_ref[slot_of(h)] for h in range(H)], axis=0)
    out_ref[...] = jnp.dot(attended.T, wo_ref[...], preferred_element_type=F32).astype(BF16)


def close(back, att_back, w_qkv, w_out):
    tok = back.shape[2]
    width = w_qkv.shape[0]
    whole = pl.BlockSpec(memory_space=pltpu.VMEM)
    return pl.pallas_call(
        close_body,
        in_specs=[whole] * 4,
        out_specs=[whole] * 2,
        out_shape=[jax.ShapeDtypeStruct((tok, width), BF16)] * 2,
        compiler_params=pltpu.CompilerParams(vmem_limit_bytes=32 * 2**20),
        cost_estimate=pl.CostEstimate(
            flops=2 * tok * width * 4 * width, bytes_accessed=8 * 2**20, transcendentals=0
        ),
        name="close",
    )(back, att_back, w_qkv, w_out)


def shards(inputs, cotangent, key_tiles, tile_valid, w_qkv, w_out):
    width = inputs.shape[2]
    x = inputs[0]
    cot = cotangent[0]
    peers = lax.axis_size("seq")
    slides = lax.axis_size("slide")
    myself = lax.axis_index("seq")
    slide = lax.axis_index("slide")
    x_all = lax.all_gather(x, "seq", axis=0)
    sent = project(x, cot, w_qkv, w_out)
    arrived = lax.all_to_all(sent, "seq", split_axis=0, concat_axis=0, tiled=True)
    group_tiles = lax.dynamic_index_in_dim(key_tiles[0], myself // 4, 0, keepdims=False)
    att_sent, low, stats = forward(group_tiles, tile_valid[0], arrived)
    att_back = lax.all_to_all(att_sent, "seq", split_axis=0, concat_axis=0, tiled=True)
    results = backward(group_tiles, arrived, low, stats)
    back = lax.all_to_all(results, "seq", split_axis=0, concat_axis=0, tiled=True)
    mine, theirs = weigh(lax.rem(slide, 2)[None], results, x_all, att_back, cot)
    got = lax.ppermute(theirs, "slide", [(i, i ^ 1) for i in range(slides)])
    keep, *sends = merge((slide // 2)[None], mine, got)
    takes = [
        lax.ppermute(send, "slide", [(i, (i + 2 * k) % slides) for i in range(slides)]).astype(F32)
        for k, send in zip((1, 2, 3), sends)
    ]
    piece = ((keep.astype(F32) + takes[1]) + (takes[0] + takes[2])).astype(BF16)
    piece, back = lax.optimization_barrier((piece, back))
    piece = piece.reshape(peers, width // peers, piece.shape[1])
    spread = lax.all_to_all(piece, "seq", split_axis=0, concat_axis=0, tiled=True)
    w_qkv_grad, w_out_grad = settle(lax.all_gather(collect(spread), "slide", axis=0))
    grad_inputs, outputs = close(back, att_back, w_qkv, w_out)
    return outputs[None], grad_inputs[None], w_qkv_grad, w_out_grad


def solution(mesh):
    placed = (
        P("slide", "seq", None),
        P("slide", "seq", None),
        P("slide", None, None, None),
        P("slide", None),
        P(),
        P(),
    )
    return jax.shard_map(
        shards,
        mesh=mesh,
        in_specs=placed,
        out_specs=(
            P("slide", "seq", None),
            P("slide", "seq", None),
            P("seq", None),
            P("seq", None),
        ),
        check_vma=False,
    )
```

```python
import jax
import jax.numpy as jnp
from jax import lax
from jax.experimental import pallas as pl
from jax.experimental.pallas import tpu as pltpu
from jax.sharding import PartitionSpec as P

H = 12
HPG = 3
HD = 64
TILE = 128
NEG_FILL = -1e30
F32 = jnp.float32
BF16 = jnp.bfloat16
SCALE = HD ** (-0.5)
NB = 4
HEADS_STEP = 4


def slot_of(head):
    row = head // HPG
    place = head % HPG
    return 4 * row + place + (place >= row)


def project_body(x_ref, cot_ref, wq_ref, wk_ref, wv_ref, wo_ref, out_ref):
    step = pl.program_id(0)
    x = x_ref[...]
    qt, kt, vt = [
        jnp.dot(x, ref[...], preferred_element_type=F32).astype(BF16).T
        for ref in (wq_ref, wk_ref, wv_ref)
    ]
    gt = lax.dot_general(
        wo_ref[...], cot_ref[...], (((1,), (1,)), ((), ())), preferred_element_type=F32
    ).astype(BF16)
    qt = qt * jnp.asarray(SCALE, BF16)
    for part in range(HEADS_STEP):
        head = HEADS_STEP * step + part
        row = head // HPG
        place = head - row * HPG
        slot = 4 * row + place + jnp.where(place >= row, 1, 0)
        rows = slice(part * HD, part * HD + HD)
        out_ref[slot, 0:HD, :] = qt[rows]
        out_ref[slot, HD : 2 * HD, :] = kt[rows]
        out_ref[slot, 2 * HD : 3 * HD, :] = vt[rows]
        out_ref[slot, 3 * HD :, :] = gt[rows]

    @pl.when(step == 0)
    def _():
        for row in range(4):
            out_ref[5 * row] = jnp.zeros(out_ref.shape[1:], BF16)


def project(x, cot, w_qkv, w_out):
    tok, width = x.shape
    steps = H // HEADS_STEP
    wide = HEADS_STEP * HD
    return pl.pallas_call(
        project_body,
        grid=(steps,),
        in_specs=[
            pl.BlockSpec((tok, width), lambda i: (0, 0)),
            pl.BlockSpec((tok, width), lambda i: (0, 0)),
            pl.BlockSpec((width, wide), lambda i: (0, i)),
            pl.BlockSpec((width, wide), lambda i: (0, i + steps)),
            pl.BlockSpec((width, wide), lambda i: (0, i + 2 * steps)),
            pl.BlockSpec((wide, width), lambda i: (i, 0)),
        ],
        out_specs=pl.BlockSpec((16, 4 * HD, tok), lambda i: (0, 0, 0)),
        out_shape=jax.ShapeDtypeStruct((16, 4 * HD, tok), BF16),
        compiler_params=pltpu.CompilerParams(vmem_limit_bytes=60 * 2**20),
        cost_estimate=pl.CostEstimate(
            flops=2 * tok * width * 4 * width, bytes_accessed=8 * 2**20, transcendentals=0
        ),
        name="project",
    )(x, cot, w_qkv, w_qkv, w_qkv, w_out)


def forward_body(tiles_ref, valid_ref, in_ref, att_ref, exp_ref, stat_ref, kv, vt):
    b = pl.program_id(0)
    blocks = in_ref.shape[0]
    listed = tiles_ref.shape[1]

    @pl.when(b == 0)
    def _():
        def prepare(i, carry):
            both = in_ref[i, HD : 3 * HD, :]
            flipped = both.T
            for c in range(2):
                vt[2 * i + c] = both[HD:, c * TILE : (c + 1) * TILE]
                kv[2 * i + c] = flipped[c * TILE : (c + 1) * TILE]
            return carry

        lax.fori_loop(0, blocks, prepare, 0)

    work = []
    for n in range(NB):
        p = NB * b + n
        tiles = [2 * p, 2 * p + 1] + [tiles_ref[p, i] for i in range(listed)]
        qt = in_ref[p, 0:HD, :]
        keys = jnp.concatenate([kv[t] for t in tiles], axis=0)
        scores = jnp.dot(
            keys, jnp.concatenate([qt, jnp.zeros_like(qt)], axis=0), preferred_element_type=F32
        )
        work.append((n, p, tiles, scores))
    for n, p, tiles, scores in work:
        gt = in_ref[p, 3 * HD :, :]
        pieces = []
        for i, t in enumerate(tiles):
            bias = jnp.where(valid_ref[t] > 0, 0.0, NEG_FILL).astype(F32)
            pieces.append(scores[i * TILE : (i + 1) * TILE] + bias)
        scores = jnp.concatenate(pieces, axis=0)
        top = jnp.max(scores, axis=0, keepdims=True)
        expo = jnp.exp(scores - top)
        share = 1.0 / jnp.sum(expo, axis=0, keepdims=True)
        low = expo.astype(BF16)
        exp_ref[n] = low
        values_t = jnp.concatenate([vt[t] for t in tiles], axis=1)
        attended = jnp.dot(values_t, low, preferred_element_type=F32) * share
        scaled = (gt.astype(F32) * share).astype(BF16)
        center = jnp.sum(attended * scaled.astype(F32), axis=0, keepdims=True)
        att_ref[p] = attended.astype(BF16)
        stat_ref[p, 0:1, :] = share
        stat_ref[p, 1:2, :] = center


def forward(tiles, valid, arrived):
    blocks, rows, tok = arrived.shape
    total = blocks * tok // TILE
    slots = 10 * TILE
    whole = pl.BlockSpec(memory_space=pltpu.VMEM)
    return pl.pallas_call(
        forward_body,
        grid=(blocks // NB,),
        in_specs=[
            pl.BlockSpec(memory_space=pltpu.SMEM),
            pl.BlockSpec(memory_space=pltpu.SMEM),
            whole,
        ],
        out_specs=[whole, pl.BlockSpec((NB, slots, tok), lambda i: (i, 0, 0)), whole],
        out_shape=[
            jax.ShapeDtypeStruct((blocks, HD, tok), BF16),
            jax.ShapeDtypeStruct((blocks, slots, tok), BF16),
            jax.ShapeDtypeStruct((blocks, 8, tok), F32),
        ],
        scratch_shapes=[
            pltpu.VMEM((total, TILE, 2 * HD), BF16),
            pltpu.VMEM((total, HD, TILE), BF16),
        ],
        compiler_params=pltpu.CompilerParams(vmem_limit_bytes=60 * 2**20),
        cost_estimate=pl.CostEstimate(
            flops=blocks * 4 * 2 * tok * slots * 2 * HD,
            bytes_accessed=14 * 2**20,
            transcendentals=blocks * tok * slots,
        ),
        name="forward",
    )(tiles, valid, arrived)


def backward_body(tiles_ref, in_ref, exp_ref, stat_ref, out_ref, kv, kt, dkv):
    b = pl.program_id(0)
    blocks = in_ref.shape[0]
    listed = tiles_ref.shape[1]

    @pl.when(b == 0)
    def _():
        def prepare(i, carry):
            both = in_ref[i, HD : 3 * HD, :]
            flipped = both.T
            for c in range(2):
                kt[2 * i + c] = both[:HD, c * TILE : (c + 1) * TILE]
                kv[2 * i + c] = flipped[c * TILE : (c + 1) * TILE]
                dkv[2 * i + c] = jnp.zeros((TILE, 2 * HD), F32)
            return carry

        lax.fori_loop(0, blocks, prepare, 0)

    work = []
    for n in range(NB):
        p = NB * b + n
        tiles = [2 * p, 2 * p + 1] + [tiles_ref[p, i] for i in range(listed)]
        gt = in_ref[p, 3 * HD :, :]
        scaled = (gt.astype(F32) * stat_ref[p, 0:1, :]).astype(BF16)
        keys = jnp.concatenate([kv[t] for t in tiles], axis=0)
        grad_probs = jnp.dot(
            keys,
            jnp.concatenate([jnp.zeros_like(scaled), scaled], axis=0),
            preferred_element_type=F32,
        )
        work.append((n, p, tiles, scaled, grad_probs))
    for n, p, tiles, scaled, grad_probs in work:
        qt = in_ref[p, 0:HD, :]
        low = exp_ref[n]
        center = stat_ref[p, 1:2, :]
        grad_scores = (low.astype(F32) * (grad_probs - center)).astype(BF16)
        keys_t = jnp.concatenate([kt[t] for t in tiles], axis=1)
        grad_q = jnp.dot(keys_t, grad_scores, preferred_element_type=F32) * SCALE
        out_ref[p, 0:HD, :] = grad_q.astype(BF16)
        flipped = jnp.concatenate([qt, scaled], axis=0).T
        lane = lax.broadcasted_iota(jnp.int32, flipped.shape, 1)
        nothing = jnp.zeros_like(flipped)
        right = jnp.concatenate(
            [jnp.where(lane < HD, flipped, nothing), jnp.where(lane < HD, nothing, flipped)],
            axis=0,
        )
        terms = jnp.dot(
            jnp.concatenate([grad_scores, low], axis=1), right, preferred_element_type=F32
        )
        for i, t in enumerate(tiles):
            dkv[t] += terms[i * TILE : (i + 1) * TILE]

    @pl.when(b == blocks // NB - 1)
    def _():
        def finish(i, carry):
            both = jnp.concatenate([dkv[2 * i], dkv[2 * i + 1]], axis=0)
            out_ref[i, HD:, :] = both.astype(BF16).T
            return carry

        lax.fori_loop(0, blocks, finish, 0)


def backward(tiles, arrived, low, stats):
    blocks, rows, tok = arrived.shape
    total = blocks * tok // TILE
    slots = 10 * TILE
    whole = pl.BlockSpec(memory_space=pltpu.VMEM)
    return pl.pallas_call(
        backward_body,
        grid=(blocks // NB,),
        in_specs=[
            pl.BlockSpec(memory_space=pltpu.SMEM),
            whole,
            pl.BlockSpec((NB, slots, tok), lambda i: (i, 0, 0)),
            whole,
        ],
        out_specs=whole,
        out_shape=jax.ShapeDtypeStruct((blocks, 3 * HD, tok), BF16),
        scratch_shapes=[
            pltpu.VMEM((total, TILE, 2 * HD), BF16),
            pltpu.VMEM((total, HD, TILE), BF16),
            pltpu.VMEM((total, TILE, 2 * HD), F32),
        ],
        compiler_params=pltpu.CompilerParams(vmem_limit_bytes=60 * 2**20),
        cost_estimate=pl.CostEstimate(
            flops=blocks * 8 * 2 * tok * slots * 2 * HD,
            bytes_accessed=16 * 2**20,
            transcendentals=0,
        ),
        name="backward",
    )(tiles, arrived, low, stats)


def weigh_body(core_ref, res_ref, x_ref, back_ref, cot_ref, mine_ref, theirs_ref, acc, out_acc):
    step = pl.program_id(0)
    part = jnp.dot(res_ref[0], x_ref[0], preferred_element_type=F32)
    for i in range(1, res_ref.shape[0]):
        part += jnp.dot(res_ref[i], x_ref[i], preferred_element_type=F32)

    @pl.when(step == 0)
    def _():
        attended = jnp.concatenate([back_ref[slot_of(h)] for h in range(H)], axis=0).T
        out_acc[...] = jnp.dot(cot_ref[...].T, attended, preferred_element_type=F32).astype(BF16)
        acc[...] = part

    @pl.when(step > 0)
    def _():
        acc[...] += part

    @pl.when(step == pl.num_programs(0) - 1)
    def _():
        out_cols = out_acc.shape[0] // 8
        in_cols = acc.shape[0] // 8
        fill = jnp.zeros((128 - out_cols - in_cols, acc.shape[1]), F32)

        def place(ref, slot, k):
            ref[slot, :out_cols, :] = out_acc[k * out_cols : (k + 1) * out_cols]
            ref[slot, out_cols:, :] = jnp.concatenate(
                [acc[k * in_cols : (k + 1) * in_cols], fill], axis=0
            ).astype(BF16)

        @pl.when(core_ref[0] == 0)
        def _():
            for k in range(4):
                place(mine_ref, k, 2 * k)
                place(theirs_ref, k, 2 * k + 1)

        @pl.when(core_ref[0] != 0)
        def _():
            for k in range(4):
                place(mine_ref, k, 2 * k + 1)
                place(theirs_ref, k, 2 * k)


def weigh(core, results, x_all, att_back, cot):
    blocks, wide, tok = results.shape
    width = x_all.shape[2]
    whole = pl.BlockSpec(memory_space=pltpu.VMEM)
    return pl.pallas_call(
        weigh_body,
        grid=(blocks // 4,),
        in_specs=[
            pl.BlockSpec(memory_space=pltpu.SMEM),
            pl.BlockSpec((4, wide, tok), lambda i: (i, 0, 0)),
            pl.BlockSpec((4, tok, width), lambda i: (i, 0, 0)),
            whole,
            whole,
        ],
        out_specs=[whole, whole],
        out_shape=[jax.ShapeDtypeStruct((4, 128, width), BF16)] * 2,
        scratch_shapes=[pltpu.VMEM((wide, width), F32), pltpu.VMEM((width, width), BF16)],
        compiler_params=pltpu.CompilerParams(vmem_limit_bytes=60 * 2**20),
        cost_estimate=pl.CostEstimate(
            flops=2 * blocks * tok * width * wide,
            bytes_accessed=10 * 2**20,
            transcendentals=0,
        ),
        name="weigh",
    )(core, results, x_all, att_back, cot)


def merge_body(chip_ref, mine_ref, got_ref, *outs):
    for k, out in enumerate(outs):
        place = lax.rem(chip_ref[0] + k, 4)
        out[...] = (mine_ref[place].astype(F32) + got_ref[place].astype(F32)).astype(BF16)


def merge(chip, mine, got):
    whole = pl.BlockSpec(memory_space=pltpu.VMEM)
    return pl.pallas_call(
        merge_body,
        in_specs=[pl.BlockSpec(memory_space=pltpu.SMEM), whole, whole],
        out_specs=[whole] * 4,
        out_shape=[jax.ShapeDtypeStruct(mine.shape[1:], BF16)] * 4,
        compiler_params=pltpu.CompilerParams(vmem_limit_bytes=16 * 2**20),
        cost_estimate=pl.CostEstimate(flops=10**6, bytes_accessed=2 * 10**6, transcendentals=0),
        name="merge",
    )(chip, mine, got)


def fold_body(a_ref, b_ref, c_ref, d_ref, out_ref):
    total = (a_ref[...].astype(F32) + c_ref[...].astype(F32)) + (
        b_ref[...].astype(F32) + d_ref[...].astype(F32)
    )
    out_ref[...] = total.astype(BF16).T


def fold(parts):
    whole = pl.BlockSpec(memory_space=pltpu.VMEM)
    return pl.pallas_call(
        fold_body,
        in_specs=[whole] * 4,
        out_specs=whole,
        out_shape=jax.ShapeDtypeStruct(parts[0].shape[::-1], BF16),
        compiler_params=pltpu.CompilerParams(vmem_limit_bytes=16 * 2**20),
        cost_estimate=pl.CostEstimate(flops=10**6, bytes_accessed=10**6, transcendentals=0),
        name="fold",
    )(*parts)


def collect_body(spread_ref, out_ref):
    in_cols = 3 * HD // 8
    out_cols = 4 * in_cols
    total = spread_ref[0].astype(F32)
    for source in range(1, spread_ref.shape[0]):
        total += spread_ref[source].astype(F32)
    ins = [spread_ref[slot_of(h), :, out_cols : out_cols + in_cols].astype(F32) for h in range(H)]
    out_ref[...] = jnp.concatenate([total[:, :out_cols]] + ins, axis=1).astype(BF16)


def collect(spread):
    whole = pl.BlockSpec(memory_space=pltpu.VMEM)
    rows = spread.shape[1]
    return pl.pallas_call(
        collect_body,
        in_specs=[whole],
        out_specs=whole,
        out_shape=jax.ShapeDtypeStruct((rows, 6 * HD), BF16),
        compiler_params=pltpu.CompilerParams(vmem_limit_bytes=16 * 2**20),
        cost_estimate=pl.CostEstimate(flops=10**6, bytes_accessed=10**6, transcendentals=0),
        name="collect",
    )(spread)


def settle_body(all_ref, in_ref, out_ref):
    in_cols = 3 * HD // 8
    out_cols = 4 * in_cols
    parts = [all_ref[k].astype(F32) for k in range(8)]
    out_ref[...] = jnp.concatenate([part[:, :out_cols] for part in parts], axis=1)
    heads = [
        jnp.concatenate(
            [part[:, out_cols + h * in_cols : out_cols + (h + 1) * in_cols] for part in parts],
            axis=1,
        )
        for h in range(H)
    ]
    in_ref[...] = jnp.concatenate(
        [head[:, m * HD : (m + 1) * HD] for m in range(3) for head in heads], axis=1
    )


def settle(gathered):
    whole = pl.BlockSpec(memory_space=pltpu.VMEM)
    rows = gathered.shape[1]
    width = H * HD
    return pl.pallas_call(
        settle_body,
        in_specs=[whole],
        out_specs=[whole, whole],
        out_shape=[
            jax.ShapeDtypeStruct((rows, 3 * width), F32),
            jax.ShapeDtypeStruct((rows, width), F32),
        ],
        compiler_params=pltpu.CompilerParams(vmem_limit_bytes=16 * 2**20),
        cost_estimate=pl.CostEstimate(flops=10**6, bytes_accessed=10**6, transcendentals=0),
        name="settle",
    )(gathered)


def close_body(back_ref, att_ref, w_ref, wo_ref, grad_ref, out_ref):
    grad = jnp.concatenate(
        [
            back_ref[slot_of(h), m * HD : (m + 1) * HD, :]
            for m in range(3)
            for h in range(H)
        ],
        axis=0,
    )
    grad_ref[...] = lax.dot_general(
        grad.T, w_ref[...], (((1,), (1,)), ((), ())), preferred_element_type=F32
    ).astype(BF16)
    attended = jnp.concatenate([att_ref[slot_of(h)] for h in range(H)], axis=0)
    out_ref[...] = jnp.dot(attended.T, wo_ref[...], preferred_element_type=F32).astype(BF16)


def close(back, att_back, w_qkv, w_out):
    tok = back.shape[2]
    width = w_qkv.shape[0]
    whole = pl.BlockSpec(memory_space=pltpu.VMEM)
    return pl.pallas_call(
        close_body,
        in_specs=[whole] * 4,
        out_specs=[whole] * 2,
        out_shape=[jax.ShapeDtypeStruct((tok, width), BF16)] * 2,
        compiler_params=pltpu.CompilerParams(vmem_limit_bytes=32 * 2**20),
        cost_estimate=pl.CostEstimate(
            flops=2 * tok * width * 4 * width, bytes_accessed=8 * 2**20, transcendentals=0
        ),
        name="close",
    )(back, att_back, w_qkv, w_out)


def shards(inputs, cotangent, key_tiles, tile_valid, w_qkv, w_out):
    width = inputs.shape[2]
    x = inputs[0]
    cot = cotangent[0]
    peers = lax.axis_size("seq")
    slides = lax.axis_size("slide")
    myself = lax.axis_index("seq")
    slide = lax.axis_index("slide")
    x_all = lax.all_gather(x, "seq", axis=0)
    sent = project(x, cot, w_qkv, w_out)
    arrived = lax.all_to_all(sent, "seq", split_axis=0, concat_axis=0, tiled=True)
    group_tiles = lax.dynamic_index_in_dim(key_tiles[0], myself // 4, 0, keepdims=False)
    att_sent, low, stats = forward(group_tiles, tile_valid[0], arrived)
    att_back = lax.all_to_all(att_sent, "seq", split_axis=0, concat_axis=0, tiled=True)
    results = backward(group_tiles, arrived, low, stats)
    back = lax.all_to_all(results, "seq", split_axis=0, concat_axis=0, tiled=True)
    mine, theirs = weigh(lax.rem(slide, 2)[None], results, x_all, att_back, cot)
    got = lax.ppermute(theirs, "slide", [(i, i ^ 1) for i in range(slides)])
    keep, *sends = merge((slide // 2)[None], mine, got)
    takes = [
        lax.ppermute(send, "slide", [(i, (i + 2 * k) % slides) for i in range(slides)])
        for k, send in zip((1, 2, 3), sends)
    ]
    piece = fold([keep] + takes)
    piece, back = lax.optimization_barrier((piece, back))
    piece = piece.reshape(peers, width // peers, piece.shape[1])
    spread = lax.all_to_all(piece, "seq", split_axis=0, concat_axis=0, tiled=True)
    w_qkv_grad, w_out_grad = settle(lax.all_gather(collect(spread), "slide", axis=0))
    grad_inputs, outputs = close(back, att_back, w_qkv, w_out)
    return outputs[None], grad_inputs[None], w_qkv_grad, w_out_grad


def solution(mesh):
    placed = (
        P("slide", "seq", None),
        P("slide", "seq", None),
        P("slide", None, None, None),
        P("slide", None),
        P(),
        P(),
    )
    return jax.shard_map(
        shards,
        mesh=mesh,
        in_specs=placed,
        out_specs=(
            P("slide", "seq", None),
            P("slide", "seq", None),
            P("seq", None),
            P("seq", None),
        ),
        check_vma=False,
    )
```

```python
import jax
import jax.numpy as jnp
from jax import lax
from jax.experimental import pallas as pl
from jax.experimental.pallas import tpu as pltpu
from jax.sharding import PartitionSpec as P

H = 12
HPG = 3
HD = 64
TILE = 128
NEG_FILL = -1e30
F32 = jnp.float32
BF16 = jnp.bfloat16
SCALE = HD ** (-0.5)
NB = 4
HEADS_STEP = 4


def slot_of(head):
    row = head // HPG
    place = head % HPG
    return 4 * row + place + (place >= row)


def project_body(x_ref, cot_ref, wq_ref, wk_ref, wv_ref, wo_ref, out_ref):
    step = pl.program_id(0)
    x = x_ref[...]
    qt, kt, vt = [
        jnp.dot(x, ref[...], preferred_element_type=F32).astype(BF16).T
        for ref in (wq_ref, wk_ref, wv_ref)
    ]
    gt = lax.dot_general(
        wo_ref[...], cot_ref[...], (((1,), (1,)), ((), ())), preferred_element_type=F32
    ).astype(BF16)
    qt = qt * jnp.asarray(SCALE, BF16)
    for part in range(HEADS_STEP):
        head = HEADS_STEP * step + part
        row = head // HPG
        place = head - row * HPG
        slot = 4 * row + place + jnp.where(place >= row, 1, 0)
        rows = slice(part * HD, part * HD + HD)
        out_ref[slot, 0:HD, :] = qt[rows]
        out_ref[slot, HD : 2 * HD, :] = kt[rows]
        out_ref[slot, 2 * HD : 3 * HD, :] = vt[rows]
        out_ref[slot, 3 * HD :, :] = gt[rows]

    @pl.when(step == 0)
    def _():
        for row in range(4):
            out_ref[5 * row] = jnp.zeros(out_ref.shape[1:], BF16)


def project(x, cot, w_qkv, w_out):
    tok, width = x.shape
    steps = H // HEADS_STEP
    wide = HEADS_STEP * HD
    return pl.pallas_call(
        project_body,
        grid=(steps,),
        in_specs=[
            pl.BlockSpec((tok, width), lambda i: (0, 0)),
            pl.BlockSpec((tok, width), lambda i: (0, 0)),
            pl.BlockSpec((width, wide), lambda i: (0, i)),
            pl.BlockSpec((width, wide), lambda i: (0, i + steps)),
            pl.BlockSpec((width, wide), lambda i: (0, i + 2 * steps)),
            pl.BlockSpec((wide, width), lambda i: (i, 0)),
        ],
        out_specs=pl.BlockSpec((16, 4 * HD, tok), lambda i: (0, 0, 0)),
        out_shape=jax.ShapeDtypeStruct((16, 4 * HD, tok), BF16),
        compiler_params=pltpu.CompilerParams(vmem_limit_bytes=60 * 2**20),
        cost_estimate=pl.CostEstimate(
            flops=2 * tok * width * 4 * width, bytes_accessed=8 * 2**20, transcendentals=0
        ),
        name="project",
    )(x, cot, w_qkv, w_qkv, w_qkv, w_out)


def forward_body(tiles_ref, valid_ref, in_ref, att_ref, exp_ref, stat_ref, kv, vt):
    b = pl.program_id(0)
    blocks = in_ref.shape[0]
    listed = tiles_ref.shape[1]

    @pl.when(b == 0)
    def _():
        def prepare(i, carry):
            both = in_ref[i, HD : 3 * HD, :]
            flipped = both.T
            for c in range(2):
                vt[2 * i + c] = both[HD:, c * TILE : (c + 1) * TILE]
                kv[2 * i + c] = flipped[c * TILE : (c + 1) * TILE]
            return carry

        lax.fori_loop(0, blocks, prepare, 0)

    work = []
    for n in range(NB):
        p = NB * b + n
        tiles = [2 * p, 2 * p + 1] + [tiles_ref[p, i] for i in range(listed)]
        qt = in_ref[p, 0:HD, :]
        keys = jnp.concatenate([kv[t] for t in tiles], axis=0)
        scores = jnp.dot(
            keys, jnp.concatenate([qt, jnp.zeros_like(qt)], axis=0), preferred_element_type=F32
        )
        work.append((n, p, tiles, scores))
    for n, p, tiles, scores in work:
        gt = in_ref[p, 3 * HD :, :]
        pieces = []
        for i, t in enumerate(tiles):
            bias = jnp.where(valid_ref[t] > 0, 0.0, NEG_FILL).astype(F32)
            pieces.append(scores[i * TILE : (i + 1) * TILE] + bias)
        scores = jnp.concatenate(pieces, axis=0)
        top = jnp.max(scores, axis=0, keepdims=True)
        expo = jnp.exp(scores - top)
        share = 1.0 / jnp.sum(expo, axis=0, keepdims=True)
        low = expo.astype(BF16)
        exp_ref[p] = low
        values_t = jnp.concatenate([vt[t] for t in tiles], axis=1)
        attended = jnp.dot(values_t, low, preferred_element_type=F32) * share
        scaled = (gt.astype(F32) * share).astype(BF16)
        center = jnp.sum(attended * scaled.astype(F32), axis=0, keepdims=True)
        att_ref[p] = attended.astype(BF16)
        stat_ref[p, 0:1, :] = share
        stat_ref[p, 1:2, :] = center


def forward(tiles, valid, arrived):
    blocks, rows, tok = arrived.shape
    total = blocks * tok // TILE
    slots = 10 * TILE
    whole = pl.BlockSpec(memory_space=pltpu.VMEM)
    return pl.pallas_call(
        forward_body,
        grid=(blocks // NB,),
        in_specs=[
            pl.BlockSpec(memory_space=pltpu.SMEM),
            pl.BlockSpec(memory_space=pltpu.SMEM),
            whole,
        ],
        out_specs=[whole] * 4,
        out_shape=[
            jax.ShapeDtypeStruct((blocks, HD, tok), BF16),
            jax.ShapeDtypeStruct((blocks, slots, tok), BF16),
            jax.ShapeDtypeStruct((blocks, 8, tok), F32),
            jax.ShapeDtypeStruct((total, TILE, 2 * HD), BF16),
        ],
        scratch_shapes=[
            pltpu.VMEM((total, HD, TILE), BF16),
        ],
        compiler_params=pltpu.CompilerParams(vmem_limit_bytes=24 * 2**20),
        cost_estimate=pl.CostEstimate(
            flops=blocks * 4 * 2 * tok * slots * 2 * HD,
            bytes_accessed=14 * 2**20,
            transcendentals=blocks * tok * slots,
        ),
        name="forward",
    )(tiles, valid, arrived)


def backward_body(tiles_ref, in_ref, exp_ref, stat_ref, kv, out_ref, kt, dkv):
    b = pl.program_id(0)
    blocks = in_ref.shape[0]
    listed = tiles_ref.shape[1]

    @pl.when(b == 0)
    def _():
        def prepare(i, carry):
            for c in range(2):
                kt[2 * i + c] = in_ref[i, HD : 2 * HD, c * TILE : (c + 1) * TILE]
                dkv[2 * i + c] = jnp.zeros((TILE, 2 * HD), F32)
            return carry

        lax.fori_loop(0, blocks, prepare, 0)

    work = []
    for n in range(NB):
        p = NB * b + n
        tiles = [2 * p, 2 * p + 1] + [tiles_ref[p, i] for i in range(listed)]
        gt = in_ref[p, 3 * HD :, :]
        scaled = (gt.astype(F32) * stat_ref[p, 0:1, :]).astype(BF16)
        keys = jnp.concatenate([kv[t] for t in tiles], axis=0)
        grad_probs = jnp.dot(
            keys,
            jnp.concatenate([jnp.zeros_like(scaled), scaled], axis=0),
            preferred_element_type=F32,
        )
        work.append((n, p, tiles, scaled, grad_probs))
    for n, p, tiles, scaled, grad_probs in work:
        qt = in_ref[p, 0:HD, :]
        low = exp_ref[p]
        center = stat_ref[p, 1:2, :]
        grad_scores = (low.astype(F32) * (grad_probs - center)).astype(BF16)
        keys_t = jnp.concatenate([kt[t] for t in tiles], axis=1)
        grad_q = jnp.dot(keys_t, grad_scores, preferred_element_type=F32) * SCALE
        out_ref[p, 0:HD, :] = grad_q.astype(BF16)
        flipped = jnp.concatenate([qt, scaled], axis=0).T
        lane = lax.broadcasted_iota(jnp.int32, flipped.shape, 1)
        nothing = jnp.zeros_like(flipped)
        right = jnp.concatenate(
            [jnp.where(lane < HD, flipped, nothing), jnp.where(lane < HD, nothing, flipped)],
            axis=0,
        )
        terms = jnp.dot(
            jnp.concatenate([grad_scores, low], axis=1), right, preferred_element_type=F32
        )
        for i, t in enumerate(tiles):
            dkv[t] += terms[i * TILE : (i + 1) * TILE]

    @pl.when(b == blocks // NB - 1)
    def _():
        def finish(i, carry):
            both = jnp.concatenate([dkv[2 * i], dkv[2 * i + 1]], axis=0)
            out_ref[i, HD:, :] = both.astype(BF16).T
            return carry

        lax.fori_loop(0, blocks, finish, 0)


def backward(tiles, arrived, low, stats, kv):
    blocks, rows, tok = arrived.shape
    total = blocks * tok // TILE
    slots = 10 * TILE
    whole = pl.BlockSpec(memory_space=pltpu.VMEM)
    return pl.pallas_call(
        backward_body,
        grid=(blocks // NB,),
        in_specs=[
            pl.BlockSpec(memory_space=pltpu.SMEM),
            whole,
            whole,
            whole,
            whole,
        ],
        out_specs=whole,
        out_shape=jax.ShapeDtypeStruct((blocks, 3 * HD, tok), BF16),
        scratch_shapes=[
            pltpu.VMEM((total, HD, TILE), BF16),
            pltpu.VMEM((total, TILE, 2 * HD), F32),
        ],
        compiler_params=pltpu.CompilerParams(vmem_limit_bytes=24 * 2**20),
        cost_estimate=pl.CostEstimate(
            flops=blocks * 8 * 2 * tok * slots * 2 * HD,
            bytes_accessed=16 * 2**20,
            transcendentals=0,
        ),
        name="backward",
    )(tiles, arrived, low, stats, kv)


def weigh_body(core_ref, res_ref, x_ref, back_ref, cot_ref, mine_ref, theirs_ref, acc, out_acc):
    step = pl.program_id(0)
    grads = jnp.concatenate([res_ref[i] for i in range(res_ref.shape[0])], axis=1)
    tokens = x_ref[...].reshape(-1, x_ref.shape[2])
    part = jnp.dot(grads, tokens, preferred_element_type=F32)

    @pl.when(step == 0)
    def _():
        attended = jnp.concatenate([back_ref[slot_of(h)] for h in range(H)], axis=0).T
        out_acc[...] = jnp.dot(cot_ref[...].T, attended, preferred_element_type=F32).astype(BF16)
        acc[...] = part

    @pl.when(step > 0)
    def _():
        acc[...] += part

    @pl.when(step == pl.num_programs(0) - 1)
    def _():
        out_cols = out_acc.shape[0] // 8
        in_cols = acc.shape[0] // 8
        fill = jnp.zeros((128 - out_cols - in_cols, acc.shape[1]), F32)

        def place(ref, slot, k):
            ref[slot, :out_cols, :] = out_acc[k * out_cols : (k + 1) * out_cols]
            ref[slot, out_cols:, :] = jnp.concatenate(
                [acc[k * in_cols : (k + 1) * in_cols], fill], axis=0
            ).astype(BF16)

        @pl.when(core_ref[0] == 0)
        def _():
            for k in range(4):
                place(mine_ref, k, 2 * k)
                place(theirs_ref, k, 2 * k + 1)

        @pl.when(core_ref[0] != 0)
        def _():
            for k in range(4):
                place(mine_ref, k, 2 * k + 1)
                place(theirs_ref, k, 2 * k)


def weigh(core, results, x_all, att_back, cot):
    blocks, wide, tok = results.shape
    width = x_all.shape[2]
    whole = pl.BlockSpec(memory_space=pltpu.VMEM)
    return pl.pallas_call(
        weigh_body,
        grid=(blocks // 4,),
        in_specs=[
            pl.BlockSpec(memory_space=pltpu.SMEM),
            pl.BlockSpec((4, wide, tok), lambda i: (i, 0, 0)),
            pl.BlockSpec((4, tok, width), lambda i: (i, 0, 0)),
            whole,
            whole,
        ],
        out_specs=[whole, whole],
        out_shape=[jax.ShapeDtypeStruct((4, 128, width), BF16)] * 2,
        scratch_shapes=[pltpu.VMEM((wide, width), F32), pltpu.VMEM((width, width), BF16)],
        compiler_params=pltpu.CompilerParams(vmem_limit_bytes=60 * 2**20),
        cost_estimate=pl.CostEstimate(
            flops=2 * blocks * tok * width * wide,
            bytes_accessed=10 * 2**20,
            transcendentals=0,
        ),
        name="weigh",
    )(core, results, x_all, att_back, cot)


def merge_body(chip_ref, mine_ref, got_ref, *outs):
    for k, out in enumerate(outs):
        place = lax.rem(chip_ref[0] + k, 4)
        out[...] = (mine_ref[place].astype(F32) + got_ref[place].astype(F32)).astype(BF16)


def merge(chip, mine, got):
    whole = pl.BlockSpec(memory_space=pltpu.VMEM)
    return pl.pallas_call(
        merge_body,
        in_specs=[pl.BlockSpec(memory_space=pltpu.SMEM), whole, whole],
        out_specs=[whole] * 4,
        out_shape=[jax.ShapeDtypeStruct(mine.shape[1:], BF16)] * 4,
        compiler_params=pltpu.CompilerParams(vmem_limit_bytes=16 * 2**20),
        cost_estimate=pl.CostEstimate(flops=10**6, bytes_accessed=2 * 10**6, transcendentals=0),
        name="merge",
    )(chip, mine, got)


def fold_body(a_ref, b_ref, c_ref, d_ref, out_ref):
    total = (a_ref[...].astype(F32) + c_ref[...].astype(F32)) + (
        b_ref[...].astype(F32) + d_ref[...].astype(F32)
    )
    out_ref[...] = total.astype(BF16).T


def fold(parts):
    whole = pl.BlockSpec(memory_space=pltpu.VMEM)
    return pl.pallas_call(
        fold_body,
        in_specs=[whole] * 4,
        out_specs=whole,
        out_shape=jax.ShapeDtypeStruct(parts[0].shape[::-1], BF16),
        compiler_params=pltpu.CompilerParams(vmem_limit_bytes=16 * 2**20),
        cost_estimate=pl.CostEstimate(flops=10**6, bytes_accessed=10**6, transcendentals=0),
        name="fold",
    )(*parts)


def collect_body(spread_ref, out_ref):
    in_cols = 3 * HD // 8
    out_cols = 4 * in_cols
    total = spread_ref[0].astype(F32)
    for source in range(1, spread_ref.shape[0]):
        total += spread_ref[source].astype(F32)
    ins = [spread_ref[slot_of(h), :, out_cols : out_cols + in_cols].astype(F32) for h in range(H)]
    out_ref[...] = jnp.concatenate([total[:, :out_cols]] + ins, axis=1).astype(BF16)


def collect(spread):
    whole = pl.BlockSpec(memory_space=pltpu.VMEM)
    rows = spread.shape[1]
    return pl.pallas_call(
        collect_body,
        in_specs=[whole],
        out_specs=whole,
        out_shape=jax.ShapeDtypeStruct((rows, 6 * HD), BF16),
        compiler_params=pltpu.CompilerParams(vmem_limit_bytes=16 * 2**20),
        cost_estimate=pl.CostEstimate(flops=10**6, bytes_accessed=10**6, transcendentals=0),
        name="collect",
    )(spread)


def settle_body(all_ref, in_ref, out_ref):
    in_cols = 3 * HD // 8
    out_cols = 4 * in_cols
    parts = [all_ref[k].astype(F32) for k in range(8)]
    out_ref[...] = jnp.concatenate([part[:, :out_cols] for part in parts], axis=1)
    heads = [
        jnp.concatenate(
            [part[:, out_cols + h * in_cols : out_cols + (h + 1) * in_cols] for part in parts],
            axis=1,
        )
        for h in range(H)
    ]
    in_ref[...] = jnp.concatenate(
        [head[:, m * HD : (m + 1) * HD] for m in range(3) for head in heads], axis=1
    )


def settle(gathered):
    whole = pl.BlockSpec(memory_space=pltpu.VMEM)
    rows = gathered.shape[1]
    width = H * HD
    return pl.pallas_call(
        settle_body,
        in_specs=[whole],
        out_specs=[whole, whole],
        out_shape=[
            jax.ShapeDtypeStruct((rows, 3 * width), F32),
            jax.ShapeDtypeStruct((rows, width), F32),
        ],
        compiler_params=pltpu.CompilerParams(vmem_limit_bytes=16 * 2**20),
        cost_estimate=pl.CostEstimate(flops=10**6, bytes_accessed=10**6, transcendentals=0),
        name="settle",
    )(gathered)


def close_body(back_ref, att_ref, w_ref, wo_ref, grad_ref, out_ref):
    grad = jnp.concatenate(
        [
            back_ref[slot_of(h), m * HD : (m + 1) * HD, :]
            for m in range(3)
            for h in range(H)
        ],
        axis=0,
    )
    grad_ref[...] = lax.dot_general(
        grad.T, w_ref[...], (((1,), (1,)), ((), ())), preferred_element_type=F32
    ).astype(BF16)
    attended = jnp.concatenate([att_ref[slot_of(h)] for h in range(H)], axis=0)
    out_ref[...] = jnp.dot(attended.T, wo_ref[...], preferred_element_type=F32).astype(BF16)


def close(back, att_back, w_qkv, w_out):
    tok = back.shape[2]
    width = w_qkv.shape[0]
    whole = pl.BlockSpec(memory_space=pltpu.VMEM)
    return pl.pallas_call(
        close_body,
        in_specs=[whole] * 4,
        out_specs=[whole] * 2,
        out_shape=[jax.ShapeDtypeStruct((tok, width), BF16)] * 2,
        compiler_params=pltpu.CompilerParams(vmem_limit_bytes=32 * 2**20),
        cost_estimate=pl.CostEstimate(
            flops=2 * tok * width * 4 * width, bytes_accessed=8 * 2**20, transcendentals=0
        ),
        name="close",
    )(back, att_back, w_qkv, w_out)


def shards(inputs, cotangent, key_tiles, tile_valid, w_qkv, w_out):
    width = inputs.shape[2]
    x = inputs[0]
    cot = cotangent[0]
    peers = lax.axis_size("seq")
    slides = lax.axis_size("slide")
    myself = lax.axis_index("seq")
    slide = lax.axis_index("slide")
    x_all = lax.all_gather(x, "seq", axis=0)
    sent = project(x, cot, w_qkv, w_out)
    arrived = lax.all_to_all(sent, "seq", split_axis=0, concat_axis=0, tiled=True)
    group_tiles = lax.dynamic_index_in_dim(key_tiles[0], myself // 4, 0, keepdims=False)
    att_sent, low, stats, kv = forward(group_tiles, tile_valid[0], arrived)
    att_back = lax.all_to_all(att_sent, "seq", split_axis=0, concat_axis=0, tiled=True)
    results = backward(group_tiles, arrived, low, stats, kv)
    back = lax.all_to_all(results, "seq", split_axis=0, concat_axis=0, tiled=True)
    mine, theirs = weigh(lax.rem(slide, 2)[None], results, x_all, att_back, cot)
    got = lax.ppermute(theirs, "slide", [(i, i ^ 1) for i in range(slides)])
    keep, *sends = merge((slide // 2)[None], mine, got)
    takes = {
        k: lax.ppermute(sends[k - 1], "slide", [(i, (i + 2 * k) % slides) for i in range(slides)])
        for k in (2, 1, 3)
    }
    piece = fold([keep, takes[1], takes[2], takes[3]])
    piece, back = lax.optimization_barrier((piece, back))
    piece = piece.reshape(peers, width // peers, piece.shape[1])
    spread = lax.all_to_all(piece, "seq", split_axis=0, concat_axis=0, tiled=True)
    w_qkv_grad, w_out_grad = settle(lax.all_gather(collect(spread), "slide", axis=0))
    grad_inputs, outputs = close(back, att_back, w_qkv, w_out)
    return outputs[None], grad_inputs[None], w_qkv_grad, w_out_grad


def solution(mesh):
    placed = (
        P("slide", "seq", None),
        P("slide", "seq", None),
        P("slide", None, None, None),
        P("slide", None),
        P(),
        P(),
    )
    return jax.shard_map(
        shards,
        mesh=mesh,
        in_specs=placed,
        out_specs=(
            P("slide", "seq", None),
            P("slide", "seq", None),
            P("seq", None),
            P("seq", None),
        ),
        check_vma=False,
    )
```

```python
import jax
import jax.numpy as jnp
from jax import lax
from jax.experimental import pallas as pl
from jax.experimental.pallas import tpu as pltpu
from jax.sharding import PartitionSpec as P

H = 12
HPG = 3
HD = 64
TILE = 128
NEG_FILL = -1e30
F32 = jnp.float32
BF16 = jnp.bfloat16
SCALE = HD ** (-0.5)
NB = 4
HEADS_STEP = 6


def slot_of(head):
    row = head // HPG
    place = head % HPG
    return 4 * row + place + (place >= row)


def project_body(x_ref, cot_ref, wq_ref, wk_ref, wv_ref, wo_ref, out_ref):
    step = pl.program_id(0)
    x = x_ref[...]
    qt, kt, vt = [
        jnp.dot(x, ref[...], preferred_element_type=F32).astype(BF16).T
        for ref in (wq_ref, wk_ref, wv_ref)
    ]
    gt = lax.dot_general(
        wo_ref[...], cot_ref[...], (((1,), (1,)), ((), ())), preferred_element_type=F32
    ).astype(BF16)
    qt = qt * jnp.asarray(SCALE, BF16)
    for part in range(HEADS_STEP):
        head = HEADS_STEP * step + part
        row = head // HPG
        place = head - row * HPG
        slot = 4 * row + place + jnp.where(place >= row, 1, 0)
        rows = slice(part * HD, part * HD + HD)
        out_ref[slot, 0:HD, :] = qt[rows]
        out_ref[slot, HD : 2 * HD, :] = kt[rows]
        out_ref[slot, 2 * HD : 3 * HD, :] = vt[rows]
        out_ref[slot, 3 * HD :, :] = gt[rows]

    @pl.when(step == 0)
    def _():
        for row in range(4):
            out_ref[5 * row] = jnp.zeros(out_ref.shape[1:], BF16)


def project(x, cot, w_qkv, w_out):
    tok, width = x.shape
    steps = H // HEADS_STEP
    wide = HEADS_STEP * HD
    return pl.pallas_call(
        project_body,
        grid=(steps,),
        in_specs=[
            pl.BlockSpec((tok, width), lambda i: (0, 0)),
            pl.BlockSpec((tok, width), lambda i: (0, 0)),
            pl.BlockSpec((width, wide), lambda i: (0, i)),
            pl.BlockSpec((width, wide), lambda i: (0, i + steps)),
            pl.BlockSpec((width, wide), lambda i: (0, i + 2 * steps)),
            pl.BlockSpec((wide, width), lambda i: (i, 0)),
        ],
        out_specs=pl.BlockSpec((16, 4 * HD, tok), lambda i: (0, 0, 0)),
        out_shape=jax.ShapeDtypeStruct((16, 4 * HD, tok), BF16),
        compiler_params=pltpu.CompilerParams(vmem_limit_bytes=60 * 2**20),
        cost_estimate=pl.CostEstimate(
            flops=2 * tok * width * 4 * width, bytes_accessed=8 * 2**20, transcendentals=0
        ),
        name="project",
    )(x, cot, w_qkv, w_qkv, w_qkv, w_out)


def forward_body(tiles_ref, valid_ref, in_ref, att_ref, exp_ref, stat_ref, kv, vt):
    b = pl.program_id(0)
    blocks = in_ref.shape[0]
    listed = tiles_ref.shape[1]

    @pl.when(b == 0)
    def _():
        def prepare(i, carry):
            both = in_ref[i, HD : 3 * HD, :]
            flipped = both.T
            for c in range(2):
                vt[2 * i + c] = both[HD:, c * TILE : (c + 1) * TILE]
                kv[2 * i + c] = flipped[c * TILE : (c + 1) * TILE]
            return carry

        lax.fori_loop(0, blocks, prepare, 0)

    work = []
    for n in range(NB):
        p = NB * b + n
        tiles = [2 * p, 2 * p + 1] + [tiles_ref[p, i] for i in range(listed)]
        qt = in_ref[p, 0:HD, :]
        keys = jnp.concatenate([kv[t] for t in tiles], axis=0)
        scores = jnp.dot(
            keys, jnp.concatenate([qt, jnp.zeros_like(qt)], axis=0), preferred_element_type=F32
        )
        work.append((n, p, tiles, scores))
    for n, p, tiles, scores in work:
        gt = in_ref[p, 3 * HD :, :]
        pieces = []
        for i, t in enumerate(tiles):
            bias = jnp.where(valid_ref[t] > 0, 0.0, NEG_FILL).astype(F32)
            pieces.append(scores[i * TILE : (i + 1) * TILE] + bias)
        scores = jnp.concatenate(pieces, axis=0)
        top = jnp.max(scores, axis=0, keepdims=True)
        expo = jnp.exp(scores - top)
        share = 1.0 / jnp.sum(expo, axis=0, keepdims=True)
        low = expo.astype(BF16)
        exp_ref[n] = low
        values_t = jnp.concatenate([vt[t] for t in tiles], axis=1)
        attended = jnp.dot(values_t, low, preferred_element_type=F32) * share
        scaled = (gt.astype(F32) * share).astype(BF16)
        center = jnp.sum(attended * scaled.astype(F32), axis=0, keepdims=True)
        att_ref[p] = attended.astype(BF16)
        stat_ref[p, 0:1, :] = share
        stat_ref[p, 1:2, :] = center


def forward(tiles, valid, arrived):
    blocks, rows, tok = arrived.shape
    total = blocks * tok // TILE
    slots = 10 * TILE
    whole = pl.BlockSpec(memory_space=pltpu.VMEM)
    return pl.pallas_call(
        forward_body,
        grid=(blocks // NB,),
        in_specs=[
            pl.BlockSpec(memory_space=pltpu.SMEM),
            pl.BlockSpec(memory_space=pltpu.SMEM),
            whole,
        ],
        out_specs=[whole, pl.BlockSpec((NB, slots, tok), lambda i: (i, 0, 0)), whole],
        out_shape=[
            jax.ShapeDtypeStruct((blocks, HD, tok), BF16),
            jax.ShapeDtypeStruct((blocks, slots, tok), BF16),
            jax.ShapeDtypeStruct((blocks, 8, tok), F32),
        ],
        scratch_shapes=[
            pltpu.VMEM((total, TILE, 2 * HD), BF16),
            pltpu.VMEM((total, HD, TILE), BF16),
        ],
        compiler_params=pltpu.CompilerParams(vmem_limit_bytes=60 * 2**20),
        cost_estimate=pl.CostEstimate(
            flops=blocks * 4 * 2 * tok * slots * 2 * HD,
            bytes_accessed=14 * 2**20,
            transcendentals=blocks * tok * slots,
        ),
        name="forward",
    )(tiles, valid, arrived)


def backward_body(tiles_ref, in_ref, exp_ref, stat_ref, out_ref, kv, kt, dkv):
    b = pl.program_id(0)
    blocks = in_ref.shape[0]
    listed = tiles_ref.shape[1]

    @pl.when(b == 0)
    def _():
        def prepare(i, carry):
            both = in_ref[i, HD : 3 * HD, :]
            flipped = both.T
            for c in range(2):
                kt[2 * i + c] = both[:HD, c * TILE : (c + 1) * TILE]
                kv[2 * i + c] = flipped[c * TILE : (c + 1) * TILE]
                dkv[2 * i + c] = jnp.zeros((TILE, 2 * HD), F32)
            return carry

        lax.fori_loop(0, blocks, prepare, 0)

    work = []
    for n in range(NB):
        p = NB * b + n
        tiles = [2 * p, 2 * p + 1] + [tiles_ref[p, i] for i in range(listed)]
        gt = in_ref[p, 3 * HD :, :]
        scaled = (gt.astype(F32) * stat_ref[p, 0:1, :]).astype(BF16)
        keys = jnp.concatenate([kv[t] for t in tiles], axis=0)
        grad_probs = jnp.dot(
            keys,
            jnp.concatenate([jnp.zeros_like(scaled), scaled], axis=0),
            preferred_element_type=F32,
        )
        work.append((n, p, tiles, scaled, grad_probs))
    for n, p, tiles, scaled, grad_probs in work:
        qt = in_ref[p, 0:HD, :]
        low = exp_ref[n]
        center = stat_ref[p, 1:2, :]
        grad_scores = (low.astype(F32) * (grad_probs - center)).astype(BF16)
        keys_t = jnp.concatenate([kt[t] for t in tiles], axis=1)
        grad_q = jnp.dot(keys_t, grad_scores, preferred_element_type=F32) * SCALE
        out_ref[p, 0:HD, :] = grad_q.astype(BF16)
        flipped = jnp.concatenate([qt, scaled], axis=0).T
        lane = lax.broadcasted_iota(jnp.int32, flipped.shape, 1)
        nothing = jnp.zeros_like(flipped)
        right = jnp.concatenate(
            [jnp.where(lane < HD, flipped, nothing), jnp.where(lane < HD, nothing, flipped)],
            axis=0,
        )
        terms = jnp.dot(
            jnp.concatenate([grad_scores, low], axis=1), right, preferred_element_type=F32
        )
        for i, t in enumerate(tiles):
            dkv[t] += terms[i * TILE : (i + 1) * TILE]

    @pl.when(b == blocks // NB - 1)
    def _():
        def finish(i, carry):
            both = jnp.concatenate([dkv[2 * i], dkv[2 * i + 1]], axis=0)
            out_ref[i, HD:, :] = both.astype(BF16).T
            return carry

        lax.fori_loop(0, blocks, finish, 0)


def backward(tiles, arrived, low, stats):
    blocks, rows, tok = arrived.shape
    total = blocks * tok // TILE
    slots = 10 * TILE
    whole = pl.BlockSpec(memory_space=pltpu.VMEM)
    return pl.pallas_call(
        backward_body,
        grid=(blocks // NB,),
        in_specs=[
            pl.BlockSpec(memory_space=pltpu.SMEM),
            whole,
            pl.BlockSpec((NB, slots, tok), lambda i: (i, 0, 0)),
            whole,
        ],
        out_specs=whole,
        out_shape=jax.ShapeDtypeStruct((blocks, 3 * HD, tok), BF16),
        scratch_shapes=[
            pltpu.VMEM((total, TILE, 2 * HD), BF16),
            pltpu.VMEM((total, HD, TILE), BF16),
            pltpu.VMEM((total, TILE, 2 * HD), F32),
        ],
        compiler_params=pltpu.CompilerParams(vmem_limit_bytes=60 * 2**20),
        cost_estimate=pl.CostEstimate(
            flops=blocks * 8 * 2 * tok * slots * 2 * HD,
            bytes_accessed=16 * 2**20,
            transcendentals=0,
        ),
        name="backward",
    )(tiles, arrived, low, stats)


def weigh_body(core_ref, res_ref, x_ref, back_ref, cot_ref, mine_ref, theirs_ref, acc, out_acc):
    step = pl.program_id(0)
    grads = jnp.concatenate([res_ref[i] for i in range(res_ref.shape[0])], axis=1)
    tokens = x_ref[...].reshape(-1, x_ref.shape[2])
    part = jnp.dot(grads, tokens, preferred_element_type=F32)

    @pl.when(step == 0)
    def _():
        attended = jnp.concatenate([back_ref[slot_of(h)] for h in range(H)], axis=0).T
        out_acc[...] = jnp.dot(cot_ref[...].T, attended, preferred_element_type=F32).astype(BF16)
        acc[...] = part

    @pl.when(step > 0)
    def _():
        acc[...] += part

    @pl.when(step == pl.num_programs(0) - 1)
    def _():
        out_cols = out_acc.shape[0] // 8
        in_cols = acc.shape[0] // 8
        fill = jnp.zeros((128 - out_cols - in_cols, acc.shape[1]), F32)

        def place(ref, slot, k):
            ref[slot, :out_cols, :] = out_acc[k * out_cols : (k + 1) * out_cols]
            ref[slot, out_cols:, :] = jnp.concatenate(
                [acc[k * in_cols : (k + 1) * in_cols], fill], axis=0
            ).astype(BF16)

        @pl.when(core_ref[0] == 0)
        def _():
            for k in range(4):
                place(mine_ref, k, 2 * k)
                place(theirs_ref, k, 2 * k + 1)

        @pl.when(core_ref[0] != 0)
        def _():
            for k in range(4):
                place(mine_ref, k, 2 * k + 1)
                place(theirs_ref, k, 2 * k)


def weigh(core, results, x_all, att_back, cot):
    blocks, wide, tok = results.shape
    width = x_all.shape[2]
    whole = pl.BlockSpec(memory_space=pltpu.VMEM)
    return pl.pallas_call(
        weigh_body,
        grid=(blocks // 8,),
        in_specs=[
            pl.BlockSpec(memory_space=pltpu.SMEM),
            pl.BlockSpec((8, wide, tok), lambda i: (i, 0, 0)),
            pl.BlockSpec((8, tok, width), lambda i: (i, 0, 0)),
            whole,
            whole,
        ],
        out_specs=[whole, whole],
        out_shape=[jax.ShapeDtypeStruct((4, 128, width), BF16)] * 2,
        scratch_shapes=[pltpu.VMEM((wide, width), F32), pltpu.VMEM((width, width), BF16)],
        compiler_params=pltpu.CompilerParams(vmem_limit_bytes=60 * 2**20),
        cost_estimate=pl.CostEstimate(
            flops=2 * blocks * tok * width * wide,
            bytes_accessed=10 * 2**20,
            transcendentals=0,
        ),
        name="weigh",
    )(core, results, x_all, att_back, cot)


def merge_body(chip_ref, mine_ref, got_ref, *outs):
    for k, out in enumerate(outs):
        place = lax.rem(chip_ref[0] + k, 4)
        out[...] = (mine_ref[place].astype(F32) + got_ref[place].astype(F32)).astype(BF16)


def merge(chip, mine, got):
    whole = pl.BlockSpec(memory_space=pltpu.VMEM)
    return pl.pallas_call(
        merge_body,
        in_specs=[pl.BlockSpec(memory_space=pltpu.SMEM), whole, whole],
        out_specs=[whole] * 4,
        out_shape=[jax.ShapeDtypeStruct(mine.shape[1:], BF16)] * 4,
        compiler_params=pltpu.CompilerParams(vmem_limit_bytes=16 * 2**20),
        cost_estimate=pl.CostEstimate(flops=10**6, bytes_accessed=2 * 10**6, transcendentals=0),
        name="merge",
    )(chip, mine, got)


def fold_body(a_ref, b_ref, c_ref, d_ref, out_ref):
    total = (a_ref[...].astype(F32) + c_ref[...].astype(F32)) + (
        b_ref[...].astype(F32) + d_ref[...].astype(F32)
    )
    out_ref[...] = total.astype(BF16).T


def fold(parts):
    whole = pl.BlockSpec(memory_space=pltpu.VMEM)
    return pl.pallas_call(
        fold_body,
        in_specs=[whole] * 4,
        out_specs=whole,
        out_shape=jax.ShapeDtypeStruct(parts[0].shape[::-1], BF16),
        compiler_params=pltpu.CompilerParams(vmem_limit_bytes=16 * 2**20),
        cost_estimate=pl.CostEstimate(flops=10**6, bytes_accessed=10**6, transcendentals=0),
        name="fold",
    )(*parts)


def collect_body(spread_ref, out_ref):
    in_cols = 3 * HD // 8
    out_cols = 4 * in_cols
    total = spread_ref[0].astype(F32)
    for source in range(1, spread_ref.shape[0]):
        total += spread_ref[source].astype(F32)
    ins = [spread_ref[slot_of(h), :, out_cols : out_cols + in_cols].astype(F32) for h in range(H)]
    out_ref[...] = jnp.concatenate([total[:, :out_cols]] + ins, axis=1).astype(BF16)


def collect(spread):
    whole = pl.BlockSpec(memory_space=pltpu.VMEM)
    rows = spread.shape[1]
    return pl.pallas_call(
        collect_body,
        in_specs=[whole],
        out_specs=whole,
        out_shape=jax.ShapeDtypeStruct((rows, 6 * HD), BF16),
        compiler_params=pltpu.CompilerParams(vmem_limit_bytes=16 * 2**20),
        cost_estimate=pl.CostEstimate(flops=10**6, bytes_accessed=10**6, transcendentals=0),
        name="collect",
    )(spread)


def settle_body(all_ref, in_ref, out_ref):
    in_cols = 3 * HD // 8
    out_cols = 4 * in_cols
    parts = [all_ref[k].astype(F32) for k in range(8)]
    out_ref[...] = jnp.concatenate([part[:, :out_cols] for part in parts], axis=1)
    heads = [
        jnp.concatenate(
            [part[:, out_cols + h * in_cols : out_cols + (h + 1) * in_cols] for part in parts],
            axis=1,
        )
        for h in range(H)
    ]
    in_ref[...] = jnp.concatenate(
        [head[:, m * HD : (m + 1) * HD] for m in range(3) for head in heads], axis=1
    )


def settle(gathered):
    whole = pl.BlockSpec(memory_space=pltpu.VMEM)
    rows = gathered.shape[1]
    width = H * HD
    return pl.pallas_call(
        settle_body,
        in_specs=[whole],
        out_specs=[whole, whole],
        out_shape=[
            jax.ShapeDtypeStruct((rows, 3 * width), F32),
            jax.ShapeDtypeStruct((rows, width), F32),
        ],
        compiler_params=pltpu.CompilerParams(vmem_limit_bytes=16 * 2**20),
        cost_estimate=pl.CostEstimate(flops=10**6, bytes_accessed=10**6, transcendentals=0),
        name="settle",
    )(gathered)


def close_body(back_ref, att_ref, w_ref, wo_ref, grad_ref, out_ref):
    grad = jnp.concatenate(
        [
            back_ref[slot_of(h), m * HD : (m + 1) * HD, :]
            for m in range(3)
            for h in range(H)
        ],
        axis=0,
    )
    grad_ref[...] = lax.dot_general(
        grad.T, w_ref[...], (((1,), (1,)), ((), ())), preferred_element_type=F32
    ).astype(BF16)
    attended = jnp.concatenate([att_ref[slot_of(h)] for h in range(H)], axis=0)
    out_ref[...] = jnp.dot(attended.T, wo_ref[...], preferred_element_type=F32).astype(BF16)


def close(back, att_back, w_qkv, w_out):
    tok = back.shape[2]
    width = w_qkv.shape[0]
    whole = pl.BlockSpec(memory_space=pltpu.VMEM)
    return pl.pallas_call(
        close_body,
        in_specs=[whole] * 4,
        out_specs=[whole] * 2,
        out_shape=[jax.ShapeDtypeStruct((tok, width), BF16)] * 2,
        compiler_params=pltpu.CompilerParams(vmem_limit_bytes=32 * 2**20),
        cost_estimate=pl.CostEstimate(
            flops=2 * tok * width * 4 * width, bytes_accessed=8 * 2**20, transcendentals=0
        ),
        name="close",
    )(back, att_back, w_qkv, w_out)


def shards(inputs, cotangent, key_tiles, tile_valid, w_qkv, w_out):
    width = inputs.shape[2]
    x = inputs[0]
    cot = cotangent[0]
    peers = lax.axis_size("seq")
    slides = lax.axis_size("slide")
    myself = lax.axis_index("seq")
    slide = lax.axis_index("slide")
    x_all = lax.all_gather(x, "seq", axis=0)
    sent = project(x, cot, w_qkv, w_out)
    arrived = lax.all_to_all(sent, "seq", split_axis=0, concat_axis=0, tiled=True)
    group_tiles = lax.dynamic_index_in_dim(key_tiles[0], myself // 4, 0, keepdims=False)
    att_sent, low, stats = forward(group_tiles, tile_valid[0], arrived)
    att_back = lax.all_to_all(att_sent, "seq", split_axis=0, concat_axis=0, tiled=True)
    results = backward(group_tiles, arrived, low, stats)
    back = lax.all_to_all(results, "seq", split_axis=0, concat_axis=0, tiled=True)
    mine, theirs = weigh(lax.rem(slide, 2)[None], results, x_all, att_back, cot)
    got = lax.ppermute(theirs, "slide", [(i, i ^ 1) for i in range(slides)])
    keep, *sends = merge((slide // 2)[None], mine, got)
    takes = [
        lax.ppermute(send, "slide", [(i, (i + 2 * k) % slides) for i in range(slides)])
        for k, send in zip((1, 2, 3), sends)
    ]
    piece = fold([keep] + takes)
    piece, back = lax.optimization_barrier((piece, back))
    piece = piece.reshape(peers, width // peers, piece.shape[1])
    spread = lax.all_to_all(piece, "seq", split_axis=0, concat_axis=0, tiled=True)
    w_qkv_grad, w_out_grad = settle(lax.all_gather(collect(spread), "slide", axis=0))
    grad_inputs, outputs = close(back, att_back, w_qkv, w_out)
    return outputs[None], grad_inputs[None], w_qkv_grad, w_out_grad


def solution(mesh):
    placed = (
        P("slide", "seq", None),
        P("slide", "seq", None),
        P("slide", None, None, None),
        P("slide", None),
        P(),
        P(),
    )
    return jax.shard_map(
        shards,
        mesh=mesh,
        in_specs=placed,
        out_specs=(
            P("slide", "seq", None),
            P("slide", "seq", None),
            P("seq", None),
            P("seq", None),
        ),
        check_vma=False,
    )
```

```python
import jax
import jax.numpy as jnp
from jax import lax
from jax.experimental import pallas as pl
from jax.experimental.pallas import tpu as pltpu
from jax.sharding import PartitionSpec as P

H = 12
HPG = 3
HD = 64
TILE = 128
NEG_FILL = -1e30
F32 = jnp.float32
BF16 = jnp.bfloat16
SCALE = HD ** (-0.5)
NB = 4
HEADS_STEP = 6


def slot_of(head):
    row = head // HPG
    place = head % HPG
    return 4 * row + place + (place >= row)


def project_body(x_ref, cot_ref, wq_ref, wk_ref, wv_ref, wo_ref, out_ref):
    step = pl.program_id(0)
    x = x_ref[...]
    qt, kt, vt = [
        jnp.dot(x, ref[...], preferred_element_type=F32).astype(BF16).T
        for ref in (wq_ref, wk_ref, wv_ref)
    ]
    gt = lax.dot_general(
        wo_ref[...], cot_ref[...], (((1,), (1,)), ((), ())), preferred_element_type=F32
    ).astype(BF16)
    qt = qt * jnp.asarray(SCALE, BF16)
    for part in range(HEADS_STEP):
        head = HEADS_STEP * step + part
        row = head // HPG
        place = head - row * HPG
        slot = 4 * row + place + jnp.where(place >= row, 1, 0)
        rows = slice(part * HD, part * HD + HD)
        out_ref[slot, 0:HD, :] = qt[rows]
        out_ref[slot, HD : 2 * HD, :] = kt[rows]
        out_ref[slot, 2 * HD : 3 * HD, :] = vt[rows]
        out_ref[slot, 3 * HD :, :] = gt[rows]

    @pl.when(step == 0)
    def _():
        for row in range(4):
            out_ref[5 * row] = jnp.zeros(out_ref.shape[1:], BF16)


def project(x, cot, w_qkv, w_out):
    tok, width = x.shape
    steps = H // HEADS_STEP
    wide = HEADS_STEP * HD
    return pl.pallas_call(
        project_body,
        grid=(steps,),
        in_specs=[
            pl.BlockSpec((tok, width), lambda i: (0, 0)),
            pl.BlockSpec((tok, width), lambda i: (0, 0)),
            pl.BlockSpec((width, wide), lambda i: (0, i)),
            pl.BlockSpec((width, wide), lambda i: (0, i + steps)),
            pl.BlockSpec((width, wide), lambda i: (0, i + 2 * steps)),
            pl.BlockSpec((wide, width), lambda i: (i, 0)),
        ],
        out_specs=pl.BlockSpec((16, 4 * HD, tok), lambda i: (0, 0, 0)),
        out_shape=jax.ShapeDtypeStruct((16, 4 * HD, tok), BF16),
        compiler_params=pltpu.CompilerParams(vmem_limit_bytes=60 * 2**20),
        cost_estimate=pl.CostEstimate(
            flops=2 * tok * width * 4 * width, bytes_accessed=8 * 2**20, transcendentals=0
        ),
        name="project",
    )(x, cot, w_qkv, w_qkv, w_qkv, w_out)


def forward_body(tiles_ref, valid_ref, in_ref, att_ref, exp_ref, stat_ref, kv, vt):
    b = pl.program_id(0)
    blocks = in_ref.shape[0]
    listed = tiles_ref.shape[1]

    @pl.when(b == 0)
    def _():
        def prepare(i, carry):
            both = in_ref[i, HD : 3 * HD, :]
            flipped = both.T
            for c in range(2):
                vt[2 * i + c] = both[HD:, c * TILE : (c + 1) * TILE]
                kv[2 * i + c] = flipped[c * TILE : (c + 1) * TILE]
            return carry

        lax.fori_loop(0, blocks, prepare, 0)

    work = []
    for n in range(NB):
        p = NB * b + n
        tiles = [2 * p, 2 * p + 1] + [tiles_ref[p, i] for i in range(listed)]
        qt = in_ref[p, 0:HD, :]
        keys = jnp.concatenate([kv[t] for t in tiles], axis=0)
        scores = jnp.dot(
            keys, jnp.concatenate([qt, jnp.zeros_like(qt)], axis=0), preferred_element_type=F32
        )
        work.append((n, p, tiles, scores))
    for n, p, tiles, scores in work:
        gt = in_ref[p, 3 * HD :, :]
        pieces = []
        for i, t in enumerate(tiles):
            bias = jnp.where(valid_ref[t] > 0, 0.0, NEG_FILL).astype(F32)
            pieces.append(scores[i * TILE : (i + 1) * TILE] + bias)
        scores = jnp.concatenate(pieces, axis=0)
        top = jnp.max(scores, axis=0, keepdims=True)
        expo = jnp.exp(scores - top)
        share = 1.0 / jnp.sum(expo, axis=0, keepdims=True)
        low = expo.astype(BF16)
        exp_ref[n] = low
        values_t = jnp.concatenate([vt[t] for t in tiles], axis=1)
        attended = jnp.dot(values_t, low, preferred_element_type=F32) * share
        scaled = (gt.astype(F32) * share).astype(BF16)
        center = jnp.sum(attended * scaled.astype(F32), axis=0, keepdims=True)
        att_ref[p] = attended.astype(BF16)
        stat_ref[p, 0:1, :] = share
        stat_ref[p, 1:2, :] = center


def forward(tiles, valid, arrived):
    blocks, rows, tok = arrived.shape
    total = blocks * tok // TILE
    slots = 10 * TILE
    whole = pl.BlockSpec(memory_space=pltpu.VMEM)
    return pl.pallas_call(
        forward_body,
        grid=(blocks // NB,),
        in_specs=[
            pl.BlockSpec(memory_space=pltpu.SMEM),
            pl.BlockSpec(memory_space=pltpu.SMEM),
            whole,
        ],
        out_specs=[whole, pl.BlockSpec((NB, slots, tok), lambda i: (i, 0, 0)), whole],
        out_shape=[
            jax.ShapeDtypeStruct((blocks, HD, tok), BF16),
            jax.ShapeDtypeStruct((blocks, slots, tok), BF16),
            jax.ShapeDtypeStruct((blocks, 8, tok), F32),
        ],
        scratch_shapes=[
            pltpu.VMEM((total, TILE, 2 * HD), BF16),
            pltpu.VMEM((total, HD, TILE), BF16),
        ],
        compiler_params=pltpu.CompilerParams(vmem_limit_bytes=50 * 2**20),
        cost_estimate=pl.CostEstimate(
            flops=blocks * 4 * 2 * tok * slots * 2 * HD,
            bytes_accessed=14 * 2**20,
            transcendentals=blocks * tok * slots,
        ),
        name="forward",
    )(tiles, valid, arrived)


def backward_body(tiles_ref, in_ref, exp_ref, stat_ref, out_ref, kv, kt, dkv):
    b = pl.program_id(0)
    blocks = in_ref.shape[0]
    listed = tiles_ref.shape[1]

    @pl.when(b == 0)
    def _():
        def prepare(i, carry):
            both = in_ref[i, HD : 3 * HD, :]
            flipped = both.T
            for c in range(2):
                kt[2 * i + c] = both[:HD, c * TILE : (c + 1) * TILE]
                kv[2 * i + c] = flipped[c * TILE : (c + 1) * TILE]
                dkv[2 * i + c] = jnp.zeros((TILE, 2 * HD), F32)
            return carry

        lax.fori_loop(0, blocks, prepare, 0)

    work = []
    for n in range(NB):
        p = NB * b + n
        tiles = [2 * p, 2 * p + 1] + [tiles_ref[p, i] for i in range(listed)]
        gt = in_ref[p, 3 * HD :, :]
        scaled = (gt.astype(F32) * stat_ref[p, 0:1, :]).astype(BF16)
        keys = jnp.concatenate([kv[t] for t in tiles], axis=0)
        grad_probs = jnp.dot(
            keys,
            jnp.concatenate([jnp.zeros_like(scaled), scaled], axis=0),
            preferred_element_type=F32,
        )
        work.append((n, p, tiles, scaled, grad_probs))
    for n, p, tiles, scaled, grad_probs in work:
        qt = in_ref[p, 0:HD, :]
        low = exp_ref[n]
        center = stat_ref[p, 1:2, :]
        grad_scores = (low.astype(F32) * (grad_probs - center)).astype(BF16)
        keys_t = jnp.concatenate([kt[t] for t in tiles], axis=1)
        grad_q = jnp.dot(keys_t, grad_scores, preferred_element_type=F32) * SCALE
        out_ref[p, 0:HD, :] = grad_q.astype(BF16)
        flipped = jnp.concatenate([qt, scaled], axis=0).T
        lane = lax.broadcasted_iota(jnp.int32, flipped.shape, 1)
        nothing = jnp.zeros_like(flipped)
        right = jnp.concatenate(
            [jnp.where(lane < HD, flipped, nothing), jnp.where(lane < HD, nothing, flipped)],
            axis=0,
        )
        terms = jnp.dot(
            jnp.concatenate([grad_scores, low], axis=1), right, preferred_element_type=F32
        )
        for i, t in enumerate(tiles):
            dkv[t] += terms[i * TILE : (i + 1) * TILE]

    @pl.when(b == blocks // NB - 1)
    def _():
        def finish(i, carry):
            both = jnp.concatenate([dkv[2 * i], dkv[2 * i + 1]], axis=0)
            out_ref[i, HD:, :] = both.astype(BF16).T
            return carry

        lax.fori_loop(0, blocks, finish, 0)


def backward(tiles, arrived, low, stats):
    blocks, rows, tok = arrived.shape
    total = blocks * tok // TILE
    slots = 10 * TILE
    whole = pl.BlockSpec(memory_space=pltpu.VMEM)
    return pl.pallas_call(
        backward_body,
        grid=(blocks // NB,),
        in_specs=[
            pl.BlockSpec(memory_space=pltpu.SMEM),
            whole,
            pl.BlockSpec((NB, slots, tok), lambda i: (i, 0, 0)),
            whole,
        ],
        out_specs=whole,
        out_shape=jax.ShapeDtypeStruct((blocks, 3 * HD, tok), BF16),
        scratch_shapes=[
            pltpu.VMEM((total, TILE, 2 * HD), BF16),
            pltpu.VMEM((total, HD, TILE), BF16),
            pltpu.VMEM((total, TILE, 2 * HD), F32),
        ],
        compiler_params=pltpu.CompilerParams(vmem_limit_bytes=56 * 2**20),
        cost_estimate=pl.CostEstimate(
            flops=blocks * 8 * 2 * tok * slots * 2 * HD,
            bytes_accessed=16 * 2**20,
            transcendentals=0,
        ),
        name="backward",
    )(tiles, arrived, low, stats)


def by_core(core, refs, write):
    mine, theirs = refs

    @pl.when(core == 0)
    def _():
        for k in range(4):
            write(mine, k, 2 * k)
            write(theirs, k, 2 * k + 1)

    @pl.when(core != 0)
    def _():
        for k in range(4):
            write(mine, k, 2 * k + 1)
            write(theirs, k, 2 * k)


def outer_body(core_ref, back_ref, cot_ref, mine_ref, theirs_ref):
    attended = jnp.concatenate([back_ref[slot_of(h)] for h in range(H)], axis=0).T
    total = jnp.dot(cot_ref[...].T, attended, preferred_element_type=F32).astype(BF16)
    cols = mine_ref.shape[1]

    def write(ref, slot, k):
        ref[slot] = total[k * cols : (k + 1) * cols]

    by_core(core_ref[0], (mine_ref, theirs_ref), write)


def outer(core, att_back, cot):
    tok, width = cot.shape
    whole = pl.BlockSpec(memory_space=pltpu.VMEM)
    return pl.pallas_call(
        outer_body,
        in_specs=[pl.BlockSpec(memory_space=pltpu.SMEM), whole, whole],
        out_specs=[whole, whole],
        out_shape=[jax.ShapeDtypeStruct((4, width // 8, width), BF16)] * 2,
        compiler_params=pltpu.CompilerParams(vmem_limit_bytes=24 * 2**20),
        cost_estimate=pl.CostEstimate(
            flops=2 * tok * width * width, bytes_accessed=2 * 2**20, transcendentals=0
        ),
        name="outer",
    )(core, att_back, cot)


def weigh_body(core_ref, res_ref, x_ref, mine_ref, theirs_ref, acc):
    step = pl.program_id(0)
    grads = jnp.concatenate([res_ref[i] for i in range(res_ref.shape[0])], axis=1)
    tokens = x_ref[...].reshape(-1, x_ref.shape[2])
    part = jnp.dot(grads, tokens, preferred_element_type=F32)

    @pl.when(step == 0)
    def _():
        acc[...] = part

    @pl.when(step > 0)
    def _():
        acc[...] += part

    @pl.when(step == pl.num_programs(0) - 1)
    def _():
        cols = acc.shape[0] // 8
        fill = jnp.zeros((mine_ref.shape[1] - cols, acc.shape[1]), F32)

        def write(ref, slot, k):
            ref[slot] = jnp.concatenate([acc[k * cols : (k + 1) * cols], fill], axis=0).astype(BF16)

        by_core(core_ref[0], (mine_ref, theirs_ref), write)


def weigh(core, results, x_all):
    blocks, wide, tok = results.shape
    width = x_all.shape[2]
    whole = pl.BlockSpec(memory_space=pltpu.VMEM)
    return pl.pallas_call(
        weigh_body,
        grid=(blocks // 8,),
        in_specs=[
            pl.BlockSpec(memory_space=pltpu.SMEM),
            pl.BlockSpec((8, wide, tok), lambda i: (i, 0, 0)),
            pl.BlockSpec((8, tok, width), lambda i: (i, 0, 0)),
        ],
        out_specs=[whole, whole],
        out_shape=[jax.ShapeDtypeStruct((4, 32, width), BF16)] * 2,
        scratch_shapes=[pltpu.VMEM((wide, width), F32)],
        compiler_params=pltpu.CompilerParams(vmem_limit_bytes=58 * 2**20),
        cost_estimate=pl.CostEstimate(
            flops=2 * blocks * tok * width * wide,
            bytes_accessed=8 * 2**20,
            transcendentals=0,
        ),
        name="weigh",
    )(core, results, x_all)


def merge_body(chip_ref, mine_out_ref, got_out_ref, mine_in_ref, got_in_ref, *outs):
    rows = mine_out_ref.shape[1]
    for k, out in enumerate(outs):
        place = lax.rem(chip_ref[0] + k, 4)
        out[:rows, :] = (
            mine_out_ref[place].astype(F32) + got_out_ref[place].astype(F32)
        ).astype(BF16)
        out[rows:, :] = (mine_in_ref[place].astype(F32) + got_in_ref[place].astype(F32)).astype(
            BF16
        )


def merge(chip, *parts):
    whole = pl.BlockSpec(memory_space=pltpu.VMEM)
    shape = (parts[0].shape[1] + parts[2].shape[1], parts[0].shape[2])
    return pl.pallas_call(
        merge_body,
        in_specs=[pl.BlockSpec(memory_space=pltpu.SMEM)] + [whole] * 4,
        out_specs=[whole] * 4,
        out_shape=[jax.ShapeDtypeStruct(shape, BF16)] * 4,
        compiler_params=pltpu.CompilerParams(vmem_limit_bytes=16 * 2**20),
        cost_estimate=pl.CostEstimate(flops=10**6, bytes_accessed=2 * 10**6, transcendentals=0),
        name="merge",
    )(chip, *parts)


def fold_body(a_ref, b_ref, c_ref, d_ref, out_ref):
    total = (a_ref[...].astype(F32) + c_ref[...].astype(F32)) + (
        b_ref[...].astype(F32) + d_ref[...].astype(F32)
    )
    out_ref[...] = total.astype(BF16).T


def fold(parts):
    whole = pl.BlockSpec(memory_space=pltpu.VMEM)
    return pl.pallas_call(
        fold_body,
        in_specs=[whole] * 4,
        out_specs=whole,
        out_shape=jax.ShapeDtypeStruct(parts[0].shape[::-1], BF16),
        compiler_params=pltpu.CompilerParams(vmem_limit_bytes=16 * 2**20),
        cost_estimate=pl.CostEstimate(flops=10**6, bytes_accessed=10**6, transcendentals=0),
        name="fold",
    )(*parts)


def collect_body(spread_ref, out_ref):
    in_cols = 3 * HD // 8
    out_cols = 4 * in_cols
    total = spread_ref[0].astype(F32)
    for source in range(1, spread_ref.shape[0]):
        total += spread_ref[source].astype(F32)
    ins = [spread_ref[slot_of(h), :, out_cols : out_cols + in_cols].astype(F32) for h in range(H)]
    out_ref[...] = jnp.concatenate([total[:, :out_cols]] + ins, axis=1).astype(BF16)


def collect(spread):
    whole = pl.BlockSpec(memory_space=pltpu.VMEM)
    rows = spread.shape[1]
    return pl.pallas_call(
        collect_body,
        in_specs=[whole],
        out_specs=whole,
        out_shape=jax.ShapeDtypeStruct((rows, 6 * HD), BF16),
        compiler_params=pltpu.CompilerParams(vmem_limit_bytes=16 * 2**20),
        cost_estimate=pl.CostEstimate(flops=10**6, bytes_accessed=10**6, transcendentals=0),
        name="collect",
    )(spread)


def settle_body(all_ref, in_ref, out_ref):
    in_cols = 3 * HD // 8
    out_cols = 4 * in_cols
    parts = [all_ref[k].astype(F32) for k in range(8)]
    out_ref[...] = jnp.concatenate([part[:, :out_cols] for part in parts], axis=1)
    heads = [
        jnp.concatenate(
            [part[:, out_cols + h * in_cols : out_cols + (h + 1) * in_cols] for part in parts],
            axis=1,
        )
        for h in range(H)
    ]
    in_ref[...] = jnp.concatenate(
        [head[:, m * HD : (m + 1) * HD] for m in range(3) for head in heads], axis=1
    )


def settle(gathered):
    whole = pl.BlockSpec(memory_space=pltpu.VMEM)
    rows = gathered.shape[1]
    width = H * HD
    return pl.pallas_call(
        settle_body,
        in_specs=[whole],
        out_specs=[whole, whole],
        out_shape=[
            jax.ShapeDtypeStruct((rows, 3 * width), F32),
            jax.ShapeDtypeStruct((rows, width), F32),
        ],
        compiler_params=pltpu.CompilerParams(vmem_limit_bytes=16 * 2**20),
        cost_estimate=pl.CostEstimate(flops=10**6, bytes_accessed=10**6, transcendentals=0),
        name="settle",
    )(gathered)


def close_body(back_ref, att_ref, w_ref, wo_ref, grad_ref, out_ref):
    grad = jnp.concatenate(
        [
            back_ref[slot_of(h), m * HD : (m + 1) * HD, :]
            for m in range(3)
            for h in range(H)
        ],
        axis=0,
    )
    grad_ref[...] = lax.dot_general(
        grad.T, w_ref[...], (((1,), (1,)), ((), ())), preferred_element_type=F32
    ).astype(BF16)
    attended = jnp.concatenate([att_ref[slot_of(h)] for h in range(H)], axis=0)
    out_ref[...] = jnp.dot(attended.T, wo_ref[...], preferred_element_type=F32).astype(BF16)


def close(back, att_back, w_qkv, w_out):
    tok = back.shape[2]
    width = w_qkv.shape[0]
    whole = pl.BlockSpec(memory_space=pltpu.VMEM)
    return pl.pallas_call(
        close_body,
        in_specs=[whole] * 4,
        out_specs=[whole] * 2,
        out_shape=[jax.ShapeDtypeStruct((tok, width), BF16)] * 2,
        compiler_params=pltpu.CompilerParams(vmem_limit_bytes=32 * 2**20),
        cost_estimate=pl.CostEstimate(
            flops=2 * tok * width * 4 * width, bytes_accessed=8 * 2**20, transcendentals=0
        ),
        name="close",
    )(back, att_back, w_qkv, w_out)


def shards(inputs, cotangent, key_tiles, tile_valid, w_qkv, w_out):
    width = inputs.shape[2]
    x = inputs[0]
    cot = cotangent[0]
    peers = lax.axis_size("seq")
    slides = lax.axis_size("slide")
    myself = lax.axis_index("seq")
    slide = lax.axis_index("slide")
    x_all = lax.all_gather(x, "seq", axis=0)
    sent = project(x, cot, w_qkv, w_out)
    arrived = lax.all_to_all(sent, "seq", split_axis=0, concat_axis=0, tiled=True)
    group_tiles = lax.dynamic_index_in_dim(key_tiles[0], myself // 4, 0, keepdims=False)
    att_sent, low, stats = forward(group_tiles, tile_valid[0], arrived)
    att_back = lax.all_to_all(att_sent, "seq", split_axis=0, concat_axis=0, tiled=True)
    results = backward(group_tiles, arrived, low, stats)
    back = lax.all_to_all(results, "seq", split_axis=0, concat_axis=0, tiled=True)
    core = lax.rem(slide, 2)[None]

    def swap(value):
        return lax.ppermute(value, "slide", [(i, i ^ 1) for i in range(slides)])

    mine_out, theirs_out = outer(core, att_back, cot)
    got_out = swap(theirs_out)
    mine_in, theirs_in = weigh(core, results, x_all)
    got_in = swap(theirs_in)
    keep, *sends = merge((slide // 2)[None], mine_out, got_out, mine_in, got_in)
    takes = [
        lax.ppermute(send, "slide", [(i, (i + 2 * k) % slides) for i in range(slides)])
        for k, send in zip((1, 2, 3), sends)
    ]
    piece = fold([keep] + takes)
    piece, back = lax.optimization_barrier((piece, back))
    piece = piece.reshape(peers, width // peers, piece.shape[1])
    spread = lax.all_to_all(piece, "seq", split_axis=0, concat_axis=0, tiled=True)
    w_qkv_grad, w_out_grad = settle(lax.all_gather(collect(spread), "slide", axis=0))
    grad_inputs, outputs = close(back, att_back, w_qkv, w_out)
    return outputs[None], grad_inputs[None], w_qkv_grad, w_out_grad


def solution(mesh):
    placed = (
        P("slide", "seq", None),
        P("slide", "seq", None),
        P("slide", None, None, None),
        P("slide", None),
        P(),
        P(),
    )
    return jax.shard_map(
        shards,
        mesh=mesh,
        in_specs=placed,
        out_specs=(
            P("slide", "seq", None),
            P("slide", "seq", None),
            P("seq", None),
            P("seq", None),
        ),
        check_vma=False,
    )
```

```python
import jax
import jax.numpy as jnp
from jax import lax
from jax.experimental import pallas as pl
from jax.experimental.pallas import tpu as pltpu
from jax.sharding import PartitionSpec as P

H = 12
HPG = 3
HD = 64
TILE = 128
NEG_FILL = -1e30
F32 = jnp.float32
BF16 = jnp.bfloat16
SCALE = HD ** (-0.5)
NB = 4
HEADS_STEP = 6


def slot_of(head):
    row = head // HPG
    place = head % HPG
    return 4 * row + place + (place >= row)


def project_body(x_ref, cot_ref, wq_ref, wk_ref, wv_ref, wo_ref, out_ref):
    step = pl.program_id(0)
    x = x_ref[...]
    qt, kt, vt = [
        jnp.dot(x, ref[...], preferred_element_type=F32).astype(BF16).T
        for ref in (wq_ref, wk_ref, wv_ref)
    ]
    gt = lax.dot_general(
        wo_ref[...], cot_ref[...], (((1,), (1,)), ((), ())), preferred_element_type=F32
    ).astype(BF16)
    qt = qt * jnp.asarray(SCALE, BF16)
    for part in range(HEADS_STEP):
        head = HEADS_STEP * step + part
        row = head // HPG
        place = head - row * HPG
        slot = 4 * row + place + jnp.where(place >= row, 1, 0)
        rows = slice(part * HD, part * HD + HD)
        out_ref[slot, 0:HD, :] = qt[rows]
        out_ref[slot, HD : 2 * HD, :] = kt[rows]
        out_ref[slot, 2 * HD : 3 * HD, :] = vt[rows]
        out_ref[slot, 3 * HD :, :] = gt[rows]

    @pl.when(step == 0)
    def _():
        for row in range(4):
            out_ref[5 * row] = jnp.zeros(out_ref.shape[1:], BF16)


def project(x, cot, w_qkv, w_out):
    tok, width = x.shape
    steps = H // HEADS_STEP
    wide = HEADS_STEP * HD
    return pl.pallas_call(
        project_body,
        grid=(steps,),
        in_specs=[
            pl.BlockSpec((tok, width), lambda i: (0, 0)),
            pl.BlockSpec((tok, width), lambda i: (0, 0)),
            pl.BlockSpec((width, wide), lambda i: (0, i)),
            pl.BlockSpec((width, wide), lambda i: (0, i + steps)),
            pl.BlockSpec((width, wide), lambda i: (0, i + 2 * steps)),
            pl.BlockSpec((wide, width), lambda i: (i, 0)),
        ],
        out_specs=pl.BlockSpec((16, 4 * HD, tok), lambda i: (0, 0, 0)),
        out_shape=jax.ShapeDtypeStruct((16, 4 * HD, tok), BF16),
        compiler_params=pltpu.CompilerParams(vmem_limit_bytes=60 * 2**20),
        cost_estimate=pl.CostEstimate(
            flops=2 * tok * width * 4 * width, bytes_accessed=8 * 2**20, transcendentals=0
        ),
        name="project",
    )(x, cot, w_qkv, w_qkv, w_qkv, w_out)


def forward_body(tiles_ref, valid_ref, in_ref, att_ref, exp_ref, stat_ref, kv, vt):
    b = pl.program_id(0)
    blocks = in_ref.shape[0]
    listed = tiles_ref.shape[1]

    @pl.when(b == 0)
    def _():
        def prepare(i, carry):
            both = in_ref[i, HD : 3 * HD, :]
            flipped = both.T
            for c in range(2):
                vt[2 * i + c] = both[HD:, c * TILE : (c + 1) * TILE]
                kv[2 * i + c] = flipped[c * TILE : (c + 1) * TILE]
            return carry

        lax.fori_loop(0, blocks, prepare, 0)

    work = []
    for n in range(NB):
        p = NB * b + n
        tiles = [2 * p, 2 * p + 1] + [tiles_ref[p, i] for i in range(listed)]
        qt = in_ref[p, 0:HD, :]
        keys = jnp.concatenate([kv[t] for t in tiles], axis=0)
        scores = jnp.dot(
            keys, jnp.concatenate([qt, jnp.zeros_like(qt)], axis=0), preferred_element_type=F32
        )
        work.append((n, p, tiles, scores))
    for n, p, tiles, scores in work:
        gt = in_ref[p, 3 * HD :, :]
        pieces = []
        for i, t in enumerate(tiles):
            bias = jnp.where(valid_ref[t] > 0, 0.0, NEG_FILL).astype(F32)
            pieces.append(scores[i * TILE : (i + 1) * TILE] + bias)
        scores = jnp.concatenate(pieces, axis=0)
        top = jnp.max(scores, axis=0, keepdims=True)
        expo = jnp.exp(scores - top)
        share = 1.0 / jnp.sum(expo, axis=0, keepdims=True)
        low = expo.astype(BF16)
        exp_ref[n] = low
        values_t = jnp.concatenate([vt[t] for t in tiles], axis=1)
        attended = jnp.dot(values_t, low, preferred_element_type=F32) * share
        scaled = (gt.astype(F32) * share).astype(BF16)
        center = jnp.sum(attended * scaled.astype(F32), axis=0, keepdims=True)
        att_ref[p] = attended.astype(BF16)
        stat_ref[p, 0:1, :] = share
        stat_ref[p, 1:2, :] = center


def forward(tiles, valid, arrived):
    blocks, rows, tok = arrived.shape
    total = blocks * tok // TILE
    slots = 10 * TILE
    whole = pl.BlockSpec(memory_space=pltpu.VMEM)
    return pl.pallas_call(
        forward_body,
        grid=(blocks // NB,),
        in_specs=[
            pl.BlockSpec(memory_space=pltpu.SMEM),
            pl.BlockSpec(memory_space=pltpu.SMEM),
            whole,
        ],
        out_specs=[whole, pl.BlockSpec((NB, slots, tok), lambda i: (i, 0, 0)), whole],
        out_shape=[
            jax.ShapeDtypeStruct((blocks, HD, tok), BF16),
            jax.ShapeDtypeStruct((blocks, slots, tok), BF16),
            jax.ShapeDtypeStruct((blocks, 8, tok), F32),
        ],
        scratch_shapes=[
            pltpu.VMEM((total, TILE, 2 * HD), BF16),
            pltpu.VMEM((total, HD, TILE), BF16),
        ],
        compiler_params=pltpu.CompilerParams(vmem_limit_bytes=50 * 2**20),
        cost_estimate=pl.CostEstimate(
            flops=blocks * 4 * 2 * tok * slots * 2 * HD,
            bytes_accessed=14 * 2**20,
            transcendentals=blocks * tok * slots,
        ),
        name="forward",
    )(tiles, valid, arrived)


def backward_body(tiles_ref, in_ref, exp_ref, stat_ref, out_ref, kv, kt, dkv):
    b = pl.program_id(0)
    blocks = in_ref.shape[0]
    listed = tiles_ref.shape[1]

    @pl.when(b == 0)
    def _():
        def prepare(i, carry):
            both = in_ref[i, HD : 3 * HD, :]
            flipped = both.T
            for c in range(2):
                kt[2 * i + c] = both[:HD, c * TILE : (c + 1) * TILE]
                kv[2 * i + c] = flipped[c * TILE : (c + 1) * TILE]
                dkv[2 * i + c] = jnp.zeros((TILE, 2 * HD), F32)
            return carry

        lax.fori_loop(0, blocks, prepare, 0)

    work = []
    for n in range(NB):
        p = NB * b + n
        tiles = [2 * p, 2 * p + 1] + [tiles_ref[p, i] for i in range(listed)]
        gt = in_ref[p, 3 * HD :, :]
        scaled = (gt.astype(F32) * stat_ref[p, 0:1, :]).astype(BF16)
        keys = jnp.concatenate([kv[t] for t in tiles], axis=0)
        grad_probs = jnp.dot(
            keys,
            jnp.concatenate([jnp.zeros_like(scaled), scaled], axis=0),
            preferred_element_type=F32,
        )
        work.append((n, p, tiles, scaled, grad_probs))
    for n, p, tiles, scaled, grad_probs in work:
        qt = in_ref[p, 0:HD, :]
        low = exp_ref[n]
        center = stat_ref[p, 1:2, :]
        grad_scores = (low.astype(F32) * (grad_probs - center)).astype(BF16)
        keys_t = jnp.concatenate([kt[t] for t in tiles], axis=1)
        grad_q = jnp.dot(keys_t, grad_scores, preferred_element_type=F32) * SCALE
        out_ref[p, 0:HD, :] = grad_q.astype(BF16)
        flipped = jnp.concatenate([qt, scaled], axis=0).T
        lane = lax.broadcasted_iota(jnp.int32, flipped.shape, 1)
        nothing = jnp.zeros_like(flipped)
        right = jnp.concatenate(
            [jnp.where(lane < HD, flipped, nothing), jnp.where(lane < HD, nothing, flipped)],
            axis=0,
        )
        terms = jnp.dot(
            jnp.concatenate([grad_scores, low], axis=1), right, preferred_element_type=F32
        )
        for i, t in enumerate(tiles):
            dkv[t] += terms[i * TILE : (i + 1) * TILE]

    @pl.when(b == blocks // NB - 1)
    def _():
        def finish(i, carry):
            both = jnp.concatenate([dkv[2 * i], dkv[2 * i + 1]], axis=0)
            out_ref[i, HD:, :] = both.astype(BF16).T
            return carry

        lax.fori_loop(0, blocks, finish, 0)


def backward(tiles, arrived, low, stats):
    blocks, rows, tok = arrived.shape
    total = blocks * tok // TILE
    slots = 10 * TILE
    whole = pl.BlockSpec(memory_space=pltpu.VMEM)
    return pl.pallas_call(
        backward_body,
        grid=(blocks // NB,),
        in_specs=[
            pl.BlockSpec(memory_space=pltpu.SMEM),
            whole,
            pl.BlockSpec((NB, slots, tok), lambda i: (i, 0, 0)),
            whole,
        ],
        out_specs=whole,
        out_shape=jax.ShapeDtypeStruct((blocks, 3 * HD, tok), BF16),
        scratch_shapes=[
            pltpu.VMEM((total, TILE, 2 * HD), BF16),
            pltpu.VMEM((total, HD, TILE), BF16),
            pltpu.VMEM((total, TILE, 2 * HD), F32),
        ],
        compiler_params=pltpu.CompilerParams(vmem_limit_bytes=50 * 2**20),
        cost_estimate=pl.CostEstimate(
            flops=blocks * 8 * 2 * tok * slots * 2 * HD,
            bytes_accessed=16 * 2**20,
            transcendentals=0,
        ),
        name="backward",
    )(tiles, arrived, low, stats)


def by_core(core, refs, write):
    mine, theirs = refs

    @pl.when(core == 0)
    def _():
        for k in range(4):
            write(mine, k, 2 * k)
            write(theirs, k, 2 * k + 1)

    @pl.when(core != 0)
    def _():
        for k in range(4):
            write(mine, k, 2 * k + 1)
            write(theirs, k, 2 * k)


def outer_body(core_ref, back_ref, cot_ref, mine_ref, theirs_ref):
    attended = jnp.concatenate([back_ref[slot_of(h)] for h in range(H)], axis=0).T
    total = jnp.dot(cot_ref[...].T, attended, preferred_element_type=F32).astype(BF16)
    cols = mine_ref.shape[1]

    def write(ref, slot, k):
        ref[slot] = total[k * cols : (k + 1) * cols]

    by_core(core_ref[0], (mine_ref, theirs_ref), write)


def outer(core, att_back, cot):
    tok, width = cot.shape
    whole = pl.BlockSpec(memory_space=pltpu.VMEM)
    return pl.pallas_call(
        outer_body,
        in_specs=[pl.BlockSpec(memory_space=pltpu.SMEM), whole, whole],
        out_specs=[whole, whole],
        out_shape=[jax.ShapeDtypeStruct((4, width // 8, width), BF16)] * 2,
        compiler_params=pltpu.CompilerParams(vmem_limit_bytes=60 * 2**20),
        cost_estimate=pl.CostEstimate(
            flops=2 * tok * width * width, bytes_accessed=2 * 2**20, transcendentals=0
        ),
        name="outer",
    )(core, att_back, cot)


def weigh_body(core_ref, res_ref, x_ref, mine_ref, theirs_ref, acc):
    step = pl.program_id(0)
    grads = jnp.concatenate([res_ref[i] for i in range(res_ref.shape[0])], axis=1)
    tokens = x_ref[...].reshape(-1, x_ref.shape[2])
    part = jnp.dot(grads, tokens, preferred_element_type=F32)

    @pl.when(step == 0)
    def _():
        acc[...] = part

    @pl.when(step > 0)
    def _():
        acc[...] += part

    @pl.when(step == pl.num_programs(0) - 1)
    def _():
        cols = acc.shape[0] // 8
        fill = jnp.zeros((mine_ref.shape[1] - cols, acc.shape[1]), F32)

        def write(ref, slot, k):
            ref[slot] = jnp.concatenate([acc[k * cols : (k + 1) * cols], fill], axis=0).astype(BF16)

        by_core(core_ref[0], (mine_ref, theirs_ref), write)


def weigh(core, results, x_all):
    blocks, wide, tok = results.shape
    width = x_all.shape[2]
    whole = pl.BlockSpec(memory_space=pltpu.VMEM)
    return pl.pallas_call(
        weigh_body,
        grid=(blocks // 8,),
        in_specs=[
            pl.BlockSpec(memory_space=pltpu.SMEM),
            pl.BlockSpec((8, wide, tok), lambda i: (i, 0, 0)),
            pl.BlockSpec((8, tok, width), lambda i: (i, 0, 0)),
        ],
        out_specs=[whole, whole],
        out_shape=[jax.ShapeDtypeStruct((4, 32, width), BF16)] * 2,
        scratch_shapes=[pltpu.VMEM((wide, width), F32)],
        compiler_params=pltpu.CompilerParams(vmem_limit_bytes=58 * 2**20),
        cost_estimate=pl.CostEstimate(
            flops=2 * blocks * tok * width * wide,
            bytes_accessed=8 * 2**20,
            transcendentals=0,
        ),
        name="weigh",
    )(core, results, x_all)


def merge_body(chip_ref, *refs):
    parts, outs, held, sems = refs[:4], refs[4:8], refs[8:12], refs[12]
    rows = held[0].shape[1]
    order = (2, 1, 3, 0)
    copies = []
    for k in order:
        place = lax.rem(chip_ref[0] + k, 4)
        copies.append(
            [
                pltpu.make_async_copy(part.at[place], hold.at[k], sems.at[k, i])
                for i, (part, hold) in enumerate(zip(parts, held))
            ]
        )
    for group in copies:
        for copy in group:
            copy.start()
    for k, group in zip(order, copies):
        for copy in group:
            copy.wait()
        mine_out, got_out, mine_in, got_in = [hold[k].astype(F32) for hold in held]
        outs[k][:rows, :] = (mine_out + got_out).astype(BF16)
        outs[k][rows:, :] = (mine_in + got_in).astype(BF16)


def merge(chip, *parts):
    whole = pl.BlockSpec(memory_space=pltpu.VMEM)
    shape = (parts[0].shape[1] + parts[2].shape[1], parts[0].shape[2])
    return pl.pallas_call(
        merge_body,
        in_specs=[pl.BlockSpec(memory_space=pltpu.SMEM)]
        + [pl.BlockSpec(memory_space=pl.ANY)] * 4,
        out_specs=[whole] * 4,
        out_shape=[jax.ShapeDtypeStruct(shape, BF16)] * 4,
        scratch_shapes=[pltpu.VMEM(part.shape, BF16) for part in parts]
        + [pltpu.SemaphoreType.DMA((4, 4))],
        compiler_params=pltpu.CompilerParams(vmem_limit_bytes=53 * 2**20),
        cost_estimate=pl.CostEstimate(flops=10**6, bytes_accessed=2 * 10**6, transcendentals=0),
        name="merge",
    )(chip, *parts)


def fold_body(a_ref, b_ref, c_ref, d_ref, out_ref):
    total = (a_ref[...].astype(F32) + c_ref[...].astype(F32)) + (
        b_ref[...].astype(F32) + d_ref[...].astype(F32)
    )
    out_ref[...] = total.astype(BF16).T


def fold(parts):
    whole = pl.BlockSpec(memory_space=pltpu.VMEM)
    return pl.pallas_call(
        fold_body,
        in_specs=[whole] * 4,
        out_specs=whole,
        out_shape=jax.ShapeDtypeStruct(parts[0].shape[::-1], BF16),
        compiler_params=pltpu.CompilerParams(vmem_limit_bytes=16 * 2**20),
        cost_estimate=pl.CostEstimate(flops=10**6, bytes_accessed=10**6, transcendentals=0),
        name="fold",
    )(*parts)


def collect_body(spread_ref, out_ref):
    in_cols = 3 * HD // 8
    out_cols = 4 * in_cols
    total = spread_ref[0].astype(F32)
    for source in range(1, spread_ref.shape[0]):
        total += spread_ref[source].astype(F32)
    ins = [spread_ref[slot_of(h), :, out_cols : out_cols + in_cols].astype(F32) for h in range(H)]
    out_ref[...] = jnp.concatenate([total[:, :out_cols]] + ins, axis=1).astype(BF16)


def collect(spread):
    whole = pl.BlockSpec(memory_space=pltpu.VMEM)
    rows = spread.shape[1]
    return pl.pallas_call(
        collect_body,
        in_specs=[whole],
        out_specs=whole,
        out_shape=jax.ShapeDtypeStruct((rows, 6 * HD), BF16),
        compiler_params=pltpu.CompilerParams(vmem_limit_bytes=16 * 2**20),
        cost_estimate=pl.CostEstimate(flops=10**6, bytes_accessed=10**6, transcendentals=0),
        name="collect",
    )(spread)


def settle_body(all_ref, in_ref, out_ref):
    in_cols = 3 * HD // 8
    out_cols = 4 * in_cols
    parts = [all_ref[k].astype(F32) for k in range(8)]
    out_ref[...] = jnp.concatenate([part[:, :out_cols] for part in parts], axis=1)
    heads = [
        jnp.concatenate(
            [part[:, out_cols + h * in_cols : out_cols + (h + 1) * in_cols] for part in parts],
            axis=1,
        )
        for h in range(H)
    ]
    in_ref[...] = jnp.concatenate(
        [head[:, m * HD : (m + 1) * HD] for m in range(3) for head in heads], axis=1
    )


def settle(gathered):
    whole = pl.BlockSpec(memory_space=pltpu.VMEM)
    rows = gathered.shape[1]
    width = H * HD
    return pl.pallas_call(
        settle_body,
        in_specs=[whole],
        out_specs=[whole, whole],
        out_shape=[
            jax.ShapeDtypeStruct((rows, 3 * width), F32),
            jax.ShapeDtypeStruct((rows, width), F32),
        ],
        compiler_params=pltpu.CompilerParams(vmem_limit_bytes=16 * 2**20),
        cost_estimate=pl.CostEstimate(flops=10**6, bytes_accessed=10**6, transcendentals=0),
        name="settle",
    )(gathered)


def close_body(back_ref, att_ref, w_ref, wo_ref, grad_ref, out_ref):
    grad = jnp.concatenate(
        [
            back_ref[slot_of(h), m * HD : (m + 1) * HD, :]
            for m in range(3)
            for h in range(H)
        ],
        axis=0,
    )
    grad_ref[...] = lax.dot_general(
        grad.T, w_ref[...], (((1,), (1,)), ((), ())), preferred_element_type=F32
    ).astype(BF16)
    attended = jnp.concatenate([att_ref[slot_of(h)] for h in range(H)], axis=0)
    out_ref[...] = jnp.dot(attended.T, wo_ref[...], preferred_element_type=F32).astype(BF16)


def close(back, att_back, w_qkv, w_out):
    tok = back.shape[2]
    width = w_qkv.shape[0]
    whole = pl.BlockSpec(memory_space=pltpu.VMEM)
    return pl.pallas_call(
        close_body,
        in_specs=[whole] * 4,
        out_specs=[whole] * 2,
        out_shape=[jax.ShapeDtypeStruct((tok, width), BF16)] * 2,
        compiler_params=pltpu.CompilerParams(vmem_limit_bytes=32 * 2**20),
        cost_estimate=pl.CostEstimate(
            flops=2 * tok * width * 4 * width, bytes_accessed=8 * 2**20, transcendentals=0
        ),
        name="close",
    )(back, att_back, w_qkv, w_out)


def shards(inputs, cotangent, key_tiles, tile_valid, w_qkv, w_out):
    width = inputs.shape[2]
    x = inputs[0]
    cot = cotangent[0]
    peers = lax.axis_size("seq")
    slides = lax.axis_size("slide")
    myself = lax.axis_index("seq")
    slide = lax.axis_index("slide")
    x_all = lax.all_gather(x, "seq", axis=0)
    sent = project(x, cot, w_qkv, w_out)
    arrived = lax.all_to_all(sent, "seq", split_axis=0, concat_axis=0, tiled=True)
    group_tiles = lax.dynamic_index_in_dim(key_tiles[0], myself // 4, 0, keepdims=False)
    att_sent, low, stats = forward(group_tiles, tile_valid[0], arrived)
    att_back = lax.all_to_all(att_sent, "seq", split_axis=0, concat_axis=0, tiled=True)
    results = backward(group_tiles, arrived, low, stats)
    back = lax.all_to_all(results, "seq", split_axis=0, concat_axis=0, tiled=True)
    core = lax.rem(slide, 2)[None]

    def swap(value):
        return lax.ppermute(value, "slide", [(i, i ^ 1) for i in range(slides)])

    mine_out, theirs_out = outer(core, att_back, cot)
    got_out = swap(theirs_out)
    mine_in, theirs_in = weigh(core, results, x_all)
    got_in = swap(theirs_in)
    keep, *sends = merge((slide // 2)[None], mine_out, got_out, mine_in, got_in)
    takes = [
        lax.ppermute(send, "slide", [(i, (i + 2 * k) % slides) for i in range(slides)])
        for k, send in zip((1, 2, 3), sends)
    ]
    piece = fold([keep] + takes)
    piece, back = lax.optimization_barrier((piece, back))
    piece = piece.reshape(peers, width // peers, piece.shape[1])
    spread = lax.all_to_all(piece, "seq", split_axis=0, concat_axis=0, tiled=True)
    w_qkv_grad, w_out_grad = settle(lax.all_gather(collect(spread), "slide", axis=0))
    grad_inputs, outputs = close(back, att_back, w_qkv, w_out)
    return outputs[None], grad_inputs[None], w_qkv_grad, w_out_grad


def solution(mesh):
    placed = (
        P("slide", "seq", None),
        P("slide", "seq", None),
        P("slide", None, None, None),
        P("slide", None),
        P(),
        P(),
    )
    return jax.shard_map(
        shards,
        mesh=mesh,
        in_specs=placed,
        out_specs=(
            P("slide", "seq", None),
            P("slide", "seq", None),
            P("seq", None),
            P("seq", None),
        ),
        check_vma=False,
    )
```

```python
import jax
import jax.numpy as jnp
from jax import lax
from jax.experimental import pallas as pl
from jax.experimental.pallas import tpu as pltpu
from jax.sharding import PartitionSpec as P

H = 12
HPG = 3
HD = 64
TILE = 128
NEG_FILL = -1e30
F32 = jnp.float32
BF16 = jnp.bfloat16
SCALE = HD ** (-0.5)
NB = 4
HEADS_STEP = 6


def slot_of(head):
    row = head // HPG
    place = head % HPG
    return 4 * row + place + (place >= row)


def project_body(x_ref, cot_ref, wq_ref, wk_ref, wv_ref, wo_ref, out_ref):
    step = pl.program_id(0)
    x = x_ref[...]
    qt, kt, vt = [
        jnp.dot(x, ref[...], preferred_element_type=F32).astype(BF16).T
        for ref in (wq_ref, wk_ref, wv_ref)
    ]
    gt = lax.dot_general(
        wo_ref[...], cot_ref[...], (((1,), (1,)), ((), ())), preferred_element_type=F32
    ).astype(BF16)
    qt = qt * jnp.asarray(SCALE, BF16)
    for part in range(HEADS_STEP):
        head = HEADS_STEP * step + part
        row = head // HPG
        place = head - row * HPG
        slot = 4 * row + place + jnp.where(place >= row, 1, 0)
        rows = slice(part * HD, part * HD + HD)
        out_ref[slot, 0:HD, :] = qt[rows]
        out_ref[slot, HD : 2 * HD, :] = kt[rows]
        out_ref[slot, 2 * HD : 3 * HD, :] = vt[rows]
        out_ref[slot, 3 * HD :, :] = gt[rows]

    @pl.when(step == 0)
    def _():
        for row in range(4):
            out_ref[5 * row] = jnp.zeros(out_ref.shape[1:], BF16)


def project(x, cot, w_qkv, w_out):
    tok, width = x.shape
    steps = H // HEADS_STEP
    wide = HEADS_STEP * HD
    return pl.pallas_call(
        project_body,
        grid=(steps,),
        in_specs=[
            pl.BlockSpec((tok, width), lambda i: (0, 0)),
            pl.BlockSpec((tok, width), lambda i: (0, 0)),
            pl.BlockSpec((width, wide), lambda i: (0, i)),
            pl.BlockSpec((width, wide), lambda i: (0, i + steps)),
            pl.BlockSpec((width, wide), lambda i: (0, i + 2 * steps)),
            pl.BlockSpec((wide, width), lambda i: (i, 0)),
        ],
        out_specs=pl.BlockSpec((16, 4 * HD, tok), lambda i: (0, 0, 0)),
        out_shape=jax.ShapeDtypeStruct((16, 4 * HD, tok), BF16),
        compiler_params=pltpu.CompilerParams(vmem_limit_bytes=60 * 2**20),
        cost_estimate=pl.CostEstimate(
            flops=2 * tok * width * 4 * width, bytes_accessed=8 * 2**20, transcendentals=0
        ),
        name="project",
    )(x, cot, w_qkv, w_qkv, w_qkv, w_out)


def forward_body(tiles_ref, valid_ref, in_ref, att_ref, exp_ref, stat_ref, kv, vt):
    b = pl.program_id(0)
    blocks = in_ref.shape[0]
    listed = tiles_ref.shape[1]

    @pl.when(b == 0)
    def _():
        def prepare(i, carry):
            both = in_ref[i, HD : 3 * HD, :]
            flipped = both.T
            for c in range(2):
                vt[2 * i + c] = both[HD:, c * TILE : (c + 1) * TILE]
                kv[2 * i + c] = flipped[c * TILE : (c + 1) * TILE]
            return carry

        lax.fori_loop(0, blocks, prepare, 0)

    work = []
    for n in range(NB):
        p = NB * b + n
        tiles = [2 * p, 2 * p + 1] + [tiles_ref[p, i] for i in range(listed)]
        qt = in_ref[p, 0:HD, :]
        keys = jnp.concatenate([kv[t] for t in tiles], axis=0)
        scores = jnp.dot(
            keys, jnp.concatenate([qt, jnp.zeros_like(qt)], axis=0), preferred_element_type=F32
        )
        work.append((n, p, tiles, scores))
    for n, p, tiles, scores in work:
        gt = in_ref[p, 3 * HD :, :]
        pieces = []
        for i, t in enumerate(tiles):
            bias = jnp.where(valid_ref[t] > 0, 0.0, NEG_FILL).astype(F32)
            pieces.append(scores[i * TILE : (i + 1) * TILE] + bias)
        scores = jnp.concatenate(pieces, axis=0)
        top = jnp.max(scores, axis=0, keepdims=True)
        expo = jnp.exp(scores - top)
        share = 1.0 / jnp.sum(expo, axis=0, keepdims=True)
        low = expo.astype(BF16)
        exp_ref[n] = low
        values_t = jnp.concatenate([vt[t] for t in tiles], axis=1)
        attended = jnp.dot(values_t, low, preferred_element_type=F32) * share
        scaled = (gt.astype(F32) * share).astype(BF16)
        center = jnp.sum(attended * scaled.astype(F32), axis=0, keepdims=True)
        att_ref[p] = attended.astype(BF16)
        stat_ref[p, 0:1, :] = share
        stat_ref[p, 1:2, :] = center


def forward(tiles, valid, arrived):
    blocks, rows, tok = arrived.shape
    total = blocks * tok // TILE
    slots = 10 * TILE
    whole = pl.BlockSpec(memory_space=pltpu.VMEM)
    return pl.pallas_call(
        forward_body,
        grid=(blocks // NB,),
        in_specs=[
            pl.BlockSpec(memory_space=pltpu.SMEM),
            pl.BlockSpec(memory_space=pltpu.SMEM),
            whole,
        ],
        out_specs=[whole, pl.BlockSpec((NB, slots, tok), lambda i: (i, 0, 0)), whole],
        out_shape=[
            jax.ShapeDtypeStruct((blocks, HD, tok), BF16),
            jax.ShapeDtypeStruct((blocks, slots, tok), BF16),
            jax.ShapeDtypeStruct((blocks, 8, tok), F32),
        ],
        scratch_shapes=[
            pltpu.VMEM((total, TILE, 2 * HD), BF16),
            pltpu.VMEM((total, HD, TILE), BF16),
        ],
        compiler_params=pltpu.CompilerParams(vmem_limit_bytes=50 * 2**20),
        cost_estimate=pl.CostEstimate(
            flops=blocks * 4 * 2 * tok * slots * 2 * HD,
            bytes_accessed=14 * 2**20,
            transcendentals=blocks * tok * slots,
        ),
        name="forward",
    )(tiles, valid, arrived)


def backward_body(tiles_ref, in_ref, exp_ref, stat_ref, out_ref, kv, kt, dkv):
    b = pl.program_id(0)
    blocks = in_ref.shape[0]
    listed = tiles_ref.shape[1]

    @pl.when(b == 0)
    def _():
        def prepare(i, carry):
            both = in_ref[i, HD : 3 * HD, :]
            flipped = both.T
            for c in range(2):
                kt[2 * i + c] = both[:HD, c * TILE : (c + 1) * TILE]
                kv[2 * i + c] = flipped[c * TILE : (c + 1) * TILE]
                dkv[2 * i + c] = jnp.zeros((TILE, 2 * HD), F32)
            return carry

        lax.fori_loop(0, blocks, prepare, 0)

    work = []
    for n in range(NB):
        p = NB * b + n
        tiles = [2 * p, 2 * p + 1] + [tiles_ref[p, i] for i in range(listed)]
        gt = in_ref[p, 3 * HD :, :]
        scaled = (gt.astype(F32) * stat_ref[p, 0:1, :]).astype(BF16)
        keys = jnp.concatenate([kv[t] for t in tiles], axis=0)
        grad_probs = jnp.dot(
            keys,
            jnp.concatenate([jnp.zeros_like(scaled), scaled], axis=0),
            preferred_element_type=F32,
        )
        work.append((n, p, tiles, scaled, grad_probs))
    for n, p, tiles, scaled, grad_probs in work:
        qt = in_ref[p, 0:HD, :]
        low = exp_ref[n]
        center = stat_ref[p, 1:2, :]
        grad_scores = (low.astype(F32) * (grad_probs - center)).astype(BF16)
        keys_t = jnp.concatenate([kt[t] for t in tiles], axis=1)
        grad_q = jnp.dot(keys_t, grad_scores, preferred_element_type=F32) * SCALE
        out_ref[p, 0:HD, :] = grad_q.astype(BF16)
        flipped = jnp.concatenate([qt, scaled], axis=0).T
        lane = lax.broadcasted_iota(jnp.int32, flipped.shape, 1)
        nothing = jnp.zeros_like(flipped)
        right = jnp.concatenate(
            [jnp.where(lane < HD, flipped, nothing), jnp.where(lane < HD, nothing, flipped)],
            axis=0,
        )
        terms = jnp.dot(
            jnp.concatenate([grad_scores, low], axis=1), right, preferred_element_type=F32
        )
        for i, t in enumerate(tiles):
            dkv[t] += terms[i * TILE : (i + 1) * TILE]

    @pl.when(b == blocks // NB - 1)
    def _():
        def finish(i, carry):
            both = jnp.concatenate([dkv[2 * i], dkv[2 * i + 1]], axis=0)
            out_ref[i, HD:, :] = both.astype(BF16).T
            return carry

        lax.fori_loop(0, blocks, finish, 0)


def backward(tiles, arrived, low, stats):
    blocks, rows, tok = arrived.shape
    total = blocks * tok // TILE
    slots = 10 * TILE
    whole = pl.BlockSpec(memory_space=pltpu.VMEM)
    return pl.pallas_call(
        backward_body,
        grid=(blocks // NB,),
        in_specs=[
            pl.BlockSpec(memory_space=pltpu.SMEM),
            whole,
            pl.BlockSpec((NB, slots, tok), lambda i: (i, 0, 0)),
            whole,
        ],
        out_specs=whole,
        out_shape=jax.ShapeDtypeStruct((blocks, 3 * HD, tok), BF16),
        scratch_shapes=[
            pltpu.VMEM((total, TILE, 2 * HD), BF16),
            pltpu.VMEM((total, HD, TILE), BF16),
            pltpu.VMEM((total, TILE, 2 * HD), F32),
        ],
        compiler_params=pltpu.CompilerParams(vmem_limit_bytes=50 * 2**20),
        cost_estimate=pl.CostEstimate(
            flops=blocks * 8 * 2 * tok * slots * 2 * HD,
            bytes_accessed=16 * 2**20,
            transcendentals=0,
        ),
        name="backward",
    )(tiles, arrived, low, stats)


def by_core(core, refs, write):
    mine, theirs = refs

    @pl.when(core == 0)
    def _():
        for k in range(4):
            write(mine, k, 2 * k)
            write(theirs, k, 2 * k + 1)

    @pl.when(core != 0)
    def _():
        for k in range(4):
            write(mine, k, 2 * k + 1)
            write(theirs, k, 2 * k)


def outer_body(core_ref, back_ref, cot_ref, mine_ref, theirs_ref):
    attended = jnp.concatenate([back_ref[slot_of(h)] for h in range(H)], axis=0).T
    total = jnp.dot(cot_ref[...].T, attended, preferred_element_type=F32).astype(BF16)
    cols = mine_ref.shape[1]

    def write(ref, slot, k):
        ref[slot] = total[k * cols : (k + 1) * cols]

    by_core(core_ref[0], (mine_ref, theirs_ref), write)


def outer(core, att_back, cot):
    tok, width = cot.shape
    whole = pl.BlockSpec(memory_space=pltpu.VMEM)
    return pl.pallas_call(
        outer_body,
        in_specs=[pl.BlockSpec(memory_space=pltpu.SMEM), whole, whole],
        out_specs=[whole, whole],
        out_shape=[jax.ShapeDtypeStruct((4, width // 8, width), BF16)] * 2,
        compiler_params=pltpu.CompilerParams(vmem_limit_bytes=60 * 2**20),
        cost_estimate=pl.CostEstimate(
            flops=2 * tok * width * width, bytes_accessed=2 * 2**20, transcendentals=0
        ),
        name="outer",
    )(core, att_back, cot)


def weigh_body(core_ref, res_ref, x_ref, mine_ref, theirs_ref, acc):
    step = pl.program_id(0)
    grads = jnp.concatenate([res_ref[i] for i in range(res_ref.shape[0])], axis=1)
    tokens = x_ref[...].reshape(-1, x_ref.shape[2])
    part = jnp.dot(grads, tokens, preferred_element_type=F32)

    @pl.when(step == 0)
    def _():
        acc[...] = part

    @pl.when(step > 0)
    def _():
        acc[...] += part

    @pl.when(step == pl.num_programs(0) - 1)
    def _():
        cols = acc.shape[0] // 8
        fill = jnp.zeros((mine_ref.shape[1] - cols, acc.shape[1]), F32)

        def write(ref, slot, k):
            ref[slot] = jnp.concatenate([acc[k * cols : (k + 1) * cols], fill], axis=0).astype(BF16)

        by_core(core_ref[0], (mine_ref, theirs_ref), write)


def weigh(core, results, x_all):
    blocks, wide, tok = results.shape
    width = x_all.shape[2]
    whole = pl.BlockSpec(memory_space=pltpu.VMEM)
    return pl.pallas_call(
        weigh_body,
        grid=(blocks // 8,),
        in_specs=[
            pl.BlockSpec(memory_space=pltpu.SMEM),
            pl.BlockSpec((8, wide, tok), lambda i: (i, 0, 0)),
            pl.BlockSpec((8, tok, width), lambda i: (i, 0, 0)),
        ],
        out_specs=[whole, whole],
        out_shape=[jax.ShapeDtypeStruct((4, 32, width), BF16)] * 2,
        scratch_shapes=[pltpu.VMEM((wide, width), F32)],
        compiler_params=pltpu.CompilerParams(vmem_limit_bytes=58 * 2**20),
        cost_estimate=pl.CostEstimate(
            flops=2 * blocks * tok * width * wide,
            bytes_accessed=8 * 2**20,
            transcendentals=0,
        ),
        name="weigh",
    )(core, results, x_all)


def merge_body(chip_ref, *refs):
    parts, outs, held, sems = refs[:4], refs[4:8], refs[8:12], refs[12]
    rows = held[0].shape[1]
    order = (2, 1, 3, 0)
    copies = []
    for k in order:
        place = lax.rem(chip_ref[0] + k, 4)
        copies.append(
            [
                pltpu.make_async_copy(part.at[place], hold.at[k], sems.at[k, i])
                for i, (part, hold) in enumerate(zip(parts, held))
            ]
        )
    for group in copies:
        for copy in group:
            copy.start()
    for k, group in zip(order, copies):
        for copy in group:
            copy.wait()
        mine_out, got_out, mine_in, got_in = [hold[k].astype(F32) for hold in held]
        outs[k][:rows, :] = (mine_out + got_out).astype(BF16)
        outs[k][rows:, :] = (mine_in + got_in).astype(BF16)


def merge(chip, *parts):
    whole = pl.BlockSpec(memory_space=pltpu.VMEM)
    shape = (parts[0].shape[1] + parts[2].shape[1], parts[0].shape[2])
    return pl.pallas_call(
        merge_body,
        in_specs=[pl.BlockSpec(memory_space=pltpu.SMEM)]
        + [pl.BlockSpec(memory_space=pl.ANY)] * 4,
        out_specs=[whole] * 4,
        out_shape=[jax.ShapeDtypeStruct(shape, BF16)] * 4,
        scratch_shapes=[pltpu.VMEM(part.shape, BF16) for part in parts]
        + [pltpu.SemaphoreType.DMA((4, 4))],
        compiler_params=pltpu.CompilerParams(vmem_limit_bytes=53 * 2**20),
        cost_estimate=pl.CostEstimate(flops=10**6, bytes_accessed=2 * 10**6, transcendentals=0),
        name="merge",
    )(chip, *parts)


def fold_body(a_ref, b_ref, c_ref, d_ref, out_ref):
    total = (a_ref[...].astype(F32) + c_ref[...].astype(F32)) + (
        b_ref[...].astype(F32) + d_ref[...].astype(F32)
    )
    out_ref[...] = total.astype(BF16).T


def fold(parts):
    whole = pl.BlockSpec(memory_space=pltpu.VMEM)
    return pl.pallas_call(
        fold_body,
        in_specs=[whole] * 4,
        out_specs=whole,
        out_shape=jax.ShapeDtypeStruct(parts[0].shape[::-1], BF16),
        compiler_params=pltpu.CompilerParams(vmem_limit_bytes=16 * 2**20),
        cost_estimate=pl.CostEstimate(flops=10**6, bytes_accessed=10**6, transcendentals=0),
        name="fold",
    )(*parts)


def collect_body(spread_ref, out_ref):
    in_cols = 3 * HD // 8
    out_cols = 4 * in_cols
    total = spread_ref[0].astype(F32)
    for source in range(1, spread_ref.shape[0]):
        total += spread_ref[source].astype(F32)
    ins = [spread_ref[slot_of(h), :, out_cols : out_cols + in_cols].astype(F32) for h in range(H)]
    out_ref[...] = jnp.concatenate([total[:, :out_cols]] + ins, axis=1).astype(BF16)


def collect(spread):
    whole = pl.BlockSpec(memory_space=pltpu.VMEM)
    rows = spread.shape[1]
    return pl.pallas_call(
        collect_body,
        in_specs=[whole],
        out_specs=whole,
        out_shape=jax.ShapeDtypeStruct((rows, 6 * HD), BF16),
        compiler_params=pltpu.CompilerParams(vmem_limit_bytes=16 * 2**20),
        cost_estimate=pl.CostEstimate(flops=10**6, bytes_accessed=10**6, transcendentals=0),
        name="collect",
    )(spread)


def settle_body(all_ref, in_ref, out_ref):
    in_cols = 3 * HD // 8
    out_cols = 4 * in_cols
    parts = [all_ref[k].astype(F32) for k in range(8)]
    out_ref[...] = jnp.concatenate([part[:, :out_cols] for part in parts], axis=1)
    heads = [
        jnp.concatenate(
            [part[:, out_cols + h * in_cols : out_cols + (h + 1) * in_cols] for part in parts],
            axis=1,
        )
        for h in range(H)
    ]
    in_ref[...] = jnp.concatenate(
        [head[:, m * HD : (m + 1) * HD] for m in range(3) for head in heads], axis=1
    )


def settle(gathered):
    whole = pl.BlockSpec(memory_space=pltpu.VMEM)
    rows = gathered.shape[1]
    width = H * HD
    return pl.pallas_call(
        settle_body,
        in_specs=[whole],
        out_specs=[whole, whole],
        out_shape=[
            jax.ShapeDtypeStruct((rows, 3 * width), F32),
            jax.ShapeDtypeStruct((rows, width), F32),
        ],
        compiler_params=pltpu.CompilerParams(vmem_limit_bytes=16 * 2**20),
        cost_estimate=pl.CostEstimate(flops=10**6, bytes_accessed=10**6, transcendentals=0),
        name="settle",
    )(gathered)


def close_body(back_ref, att_ref, w_ref, wo_ref, grad_ref, out_ref):
    grad = jnp.concatenate(
        [
            back_ref[slot_of(h), m * HD : (m + 1) * HD, :]
            for m in range(3)
            for h in range(H)
        ],
        axis=0,
    )
    grad_ref[...] = lax.dot_general(
        grad.T, w_ref[...], (((1,), (1,)), ((), ())), preferred_element_type=F32
    ).astype(BF16)
    attended = jnp.concatenate([att_ref[slot_of(h)] for h in range(H)], axis=0)
    out_ref[...] = jnp.dot(attended.T, wo_ref[...], preferred_element_type=F32).astype(BF16)


def close(back, att_back, w_qkv, w_out):
    tok = back.shape[2]
    width = w_qkv.shape[0]
    whole = pl.BlockSpec(memory_space=pltpu.VMEM)
    return pl.pallas_call(
        close_body,
        in_specs=[whole] * 4,
        out_specs=[whole] * 2,
        out_shape=[jax.ShapeDtypeStruct((tok, width), BF16)] * 2,
        compiler_params=pltpu.CompilerParams(vmem_limit_bytes=32 * 2**20),
        cost_estimate=pl.CostEstimate(
            flops=2 * tok * width * 4 * width, bytes_accessed=8 * 2**20, transcendentals=0
        ),
        name="close",
    )(back, att_back, w_qkv, w_out)


def shards(inputs, cotangent, key_tiles, tile_valid, w_qkv, w_out):
    width = inputs.shape[2]
    x = inputs[0]
    cot = cotangent[0]
    peers = lax.axis_size("seq")
    slides = lax.axis_size("slide")
    myself = lax.axis_index("seq")
    slide = lax.axis_index("slide")
    x_all = lax.all_gather(x, "seq", axis=0)
    sent = project(x, cot, w_qkv, w_out)
    arrived = lax.all_to_all(sent, "seq", split_axis=0, concat_axis=0, tiled=True)
    group_tiles = lax.dynamic_index_in_dim(key_tiles[0], myself // 4, 0, keepdims=False)
    att_sent, low, stats = forward(group_tiles, tile_valid[0], arrived)
    att_back = lax.all_to_all(att_sent, "seq", split_axis=0, concat_axis=0, tiled=True)
    results = backward(group_tiles, arrived, low, stats)
    core = lax.rem(slide, 2)[None]

    def swap(value):
        return lax.ppermute(value, "slide", [(i, i ^ 1) for i in range(slides)])

    mine_out, theirs_out = outer(core, att_back, cot)
    results, theirs_out = lax.optimization_barrier((results, theirs_out))
    back = lax.all_to_all(results, "seq", split_axis=0, concat_axis=0, tiled=True)
    got_out = swap(theirs_out)
    mine_in, theirs_in = weigh(core, results, x_all)
    got_in = swap(theirs_in)
    keep, *sends = merge((slide // 2)[None], mine_out, got_out, mine_in, got_in)
    takes = [
        lax.ppermute(send, "slide", [(i, (i + 2 * k) % slides) for i in range(slides)])
        for k, send in zip((1, 2, 3), sends)
    ]
    piece = fold([keep] + takes)
    piece, back = lax.optimization_barrier((piece, back))
    piece = piece.reshape(peers, width // peers, piece.shape[1])
    spread = lax.all_to_all(piece, "seq", split_axis=0, concat_axis=0, tiled=True)
    w_qkv_grad, w_out_grad = settle(lax.all_gather(collect(spread), "slide", axis=0))
    grad_inputs, outputs = close(back, att_back, w_qkv, w_out)
    return outputs[None], grad_inputs[None], w_qkv_grad, w_out_grad


def solution(mesh):
    placed = (
        P("slide", "seq", None),
        P("slide", "seq", None),
        P("slide", None, None, None),
        P("slide", None),
        P(),
        P(),
    )
    return jax.shard_map(
        shards,
        mesh=mesh,
        in_specs=placed,
        out_specs=(
            P("slide", "seq", None),
            P("slide", "seq", None),
            P("seq", None),
            P("seq", None),
        ),
        check_vma=False,
    )
```
